32 devices in a mesh: dp: 16 (over z, y, core), seq: 2 (over x).
Axes of the slice: x: 2, y: 2, z: 4, core: 2. Of those that a mesh axis runs over, the one named last changes fastest.
Arguments:
- tokens: bfloat16 [16, 322, 1152], P('dp', 'seq'), may hold values from -6 to 6
- skip_feats: bfloat16 [16, 322, 1152], P('dp', None, 'seq'), may hold values from -6 to 6
- lengths: int32 [16], P('dp'), may hold values from 194 to 322, as said below
- cotangent: bfloat16 [16, 322, 1152], P('dp', 'seq'), may hold values from -6 to 6
- skip_weight: bfloat16 [2304, 1152], replicated, may hold values from -0.125 to 0.125
- skip_bias: bfloat16 [1152], replicated, may hold values from -2 to 2
- norm1_gain: bfloat16 [1152], replicated, may hold values from 0.099609375 to 1.8984375
- norm1_bias: bfloat16 [1152], replicated, may hold values from -2 to 2
- qkv_weight: bfloat16 [1152, 3456], replicated, may hold values from -0.1875 to 0.1875
- proj_weight: bfloat16 [1152, 1152], replicated, may hold values from -1.5 to 1.5
- proj_bias: bfloat16 [1152], replicated, may hold values from -2 to 2
- norm2_gain: bfloat16 [1152], replicated, may hold values from 0.099609375 to 1.8984375
- norm2_bias: bfloat16 [1152], replicated, may hold values from -2 to 2
- fc1_weight: bfloat16 [1152, 4608], replicated, may hold values from -0.1875 to 0.1875
- fc1_bias: bfloat16 [4608], replicated, may hold values from -2 to 2
- fc2_weight: bfloat16 [4608, 1152], replicated, may hold values from -0.09375 to 0.09375
- fc2_bias: bfloat16 [1152], replicated, may hold values from -2 to 2
Outputs:
- block_out: bfloat16 [16, 322, 1152], P('dp', 'seq')
- tokens_grad: bfloat16 [16, 322, 1152], P('dp', 'seq')
- skip_grad: bfloat16 [16, 322, 1152], P('dp', None, 'seq')
- skip_weight_grad: float32 [2304, 1152], P(('dp', 'seq'))
- skip_bias_grad: float32 [1152], P(('dp', 'seq'))
- norm1_gain_grad: float32 [1152], P(('dp', 'seq'))
- norm1_bias_grad: float32 [1152], P(('dp', 'seq'))
- qkv_weight_grad: float32 [1152, 3456], P(('dp', 'seq'))
- proj_weight_grad: float32 [1152, 1152], P(('dp', 'seq'))
- proj_bias_grad: float32 [1152], P(('dp', 'seq'))
- norm2_gain_grad: float32 [1152], P(('dp', 'seq'))
- norm2_bias_grad: float32 [1152], P(('dp', 'seq'))
- fc1_weight_grad: float32 [1152, 4608], P(('dp', 'seq'))
- fc1_bias_grad: float32 [4608], P(('dp', 'seq'))
- fc2_weight_grad: float32 [4608, 1152], P(('dp', 'seq'))
- fc2_bias_grad: float32 [1152], P(('dp', 'seq'))
The draws below stay inside these ranges and needn't reach their ends.
Inputs may be any that keep to these rules, and one draw needn't show every extreme that they name: `lengths`: slots of an item at or beyond its length are padding. Some item uses all 322 slots in every draw, and some item uses the fewest.
All inputs are finite; a program needn't handle non-finite values.
Results may differ from the reference program's by a relative error of at most 0.015.
Values may be sent and summed in bfloat16 or wider, within the bound.
A program may use at most 192 MiB of HBM per device.

```python
import jax
import jax.numpy as jnp
from jax import lax

D = 1152
HEADS = 16
HEAD_DIM = 72
FF = 4608
SLOTS = 322
ITEMS_DEV = 1
ITEMS = 16
N_SEQ = 2


def draw_lengths(key, part):
    key = jax.random.fold_in(key, 11)
    shortest = max(SLOTS - 128, SLOTS // 2)
    first_key, pick_key = jax.random.split(key)
    counts = jax.random.randint(first_key, (ITEMS,), shortest, SLOTS + 1)
    chosen = jax.random.randint(pick_key, (), 0, ITEMS)
    counts = counts.at[chosen].set(SLOTS)
    counts = counts.at[(chosen + ITEMS // 2) % ITEMS].set(shortest)
    return counts.astype(jnp.int32)


def level_of(key, extent, cuts, least, top_value):
    loudness, own = 1.0, jax.random.fold_in(key, 6)
    for dim, blocks in cuts:
        heights = jnp.exp(jax.random.uniform(jax.random.fold_in(own, dim), (blocks,), jnp.float32, least / len(cuts), top_value / len(cuts)))
        loudness = loudness * jnp.repeat(heights, extent[dim] // blocks).reshape([-1 if axis == dim else 1 for axis in range(len(extent))])
    return loudness


def noise(key, extent, spread, limit, cuts=(), kind=jnp.bfloat16):
    array = spread * jax.random.normal(key, extent, jnp.float32)
    if cuts:
        array = array * level_of(key, extent, cuts, -0.22, 0.18)
    return jnp.clip(array, -limit, limit).astype(kind)


def setup_inputs(seed: int = 0) -> dict:
    keys = jax.random.split(jax.random.key(seed), 18)
    return {
        "tokens": noise(keys[0], (ITEMS, SLOTS, D), 1.0, 6.0, ((0, 16), (1, 2))),
        "skip_feats": noise(keys[1], (ITEMS, SLOTS, D), 1.0, 6.0, ((0, 16), (2, 2))),
        "lengths": draw_lengths(jax.random.fold_in(keys[17], 71), 0),
        "cotangent": noise(keys[3], (ITEMS, SLOTS, D), 1.0, 6.0, ((0, 16), (1, 2))),
        "skip_weight": noise(keys[4], (2 * D, D), (2 * D) ** -0.5, 0.125),
        "skip_bias": noise(keys[5], (D,), 0.3, 2.0),
        "norm1_gain": jnp.clip(1.0 + 0.18 * jax.random.normal(keys[6], (D,), jnp.float32), 0.099609375, 1.8984375).astype(jnp.bfloat16),
        "norm1_bias": noise(keys[7], (D,), 0.3, 2.0),
        "qkv_weight": noise(keys[8], (D, 3 * D), D ** -0.5, 0.1875),
        "proj_weight": noise(keys[9], (D, D), (4 * D // SLOTS) ** -0.5, 1.5),
        "proj_bias": noise(keys[10], (D,), 0.3, 2.0),
        "norm2_gain": jnp.clip(1.0 + 0.18 * jax.random.normal(keys[11], (D,), jnp.float32), 0.099609375, 1.8984375).astype(jnp.bfloat16),
        "norm2_bias": noise(keys[12], (D,), 0.3, 2.0),
        "fc1_weight": noise(keys[13], (D, FF), D ** -0.5, 0.1875),
        "fc1_bias": noise(keys[14], (FF,), 0.3, 2.0),
        "fc2_weight": noise(keys[15], (FF, D), FF ** -0.5, 0.09375),
        "fc2_bias": noise(keys[16], (D,), 0.3, 2.0),
    }


NORM_EPS = 1e-05
PRECISE = lax.Precision.HIGHEST

@jax.custom_vjp
def low(v):
    return lax.optimization_barrier(v.astype(jnp.bfloat16)).astype(jnp.float32)

@jax.custom_vjp
def low_back(v):
    return v

def low_keep(v):
    return (low(v), None)

def low_pass(kept, grad):
    return (grad,)

def back_keep(v):
    return (v, None)

def back_low(kept, grad):
    return (low(grad),)
low.defvjp(low_keep, low_pass)
low_back.defvjp(back_keep, back_low)

def layer_norm(v, gain, bias):
    row_mean = lax.optimization_barrier(jnp.mean(v, axis=-1, keepdims=True))
    centred = v - row_mean
    variance = lax.optimization_barrier(jnp.mean(centred * centred, axis=-1, keepdims=True))
    return centred * lax.rsqrt(variance + NORM_EPS) * gain + bias

def project(left, right):
    return jnp.einsum('gsc,cd->gsd', left, right, precision=PRECISE)

def forward(params, token_block, skip_block, row_valid):
    skip_weight, skip_bias, norm1_gain, norm1_bias, qkv_weight, proj_weight, proj_bias, norm2_gain, norm2_bias, fc1_weight, fc1_bias, fc2_weight, fc2_bias = params
    item_count, slot_count, width = token_block.shape
    joined = jnp.concatenate([token_block, skip_block], axis=-1)
    base_sum = low_back(project(joined, skip_weight)) + skip_bias
    normed = low(layer_norm(base_sum, norm1_gain, norm1_bias))
    packed = low(low_back(project(normed, qkv_weight)))
    four_d = (item_count, slot_count, HEADS, HEAD_DIM)
    query = packed[..., :width].reshape(four_d)
    key_rows = packed[..., width:2 * width].reshape(four_d)
    value_rows = packed[..., 2 * width:].reshape(four_d)
    run_length = slot_count // N_SEQ
    runs = []
    for run_index in range(N_SEQ):
        query_run = query[:, run_index * run_length:(run_index + 1) * run_length]
        key_run = low_back(key_rows)
        value_run = low_back(value_rows)
        raw_scores = low_back(jnp.einsum('gqhd,gkhd->ghqk', query_run, key_run, precision=PRECISE))
        scores = jnp.where(row_valid[:, None, None, :] > 0, raw_scores * HEAD_DIM ** (-0.5), -1e+30)
        attn_probs = jax.nn.softmax(scores, axis=-1)
        runs.append(jnp.einsum('ghqk,gkhd->gqhd', low(attn_probs), value_run, precision=PRECISE))
    head_out = jnp.concatenate(runs, axis=1)
    head_out = low(low_back(head_out.reshape(item_count, slot_count, width)))
    middle = base_sum + low_back(project(head_out, proj_weight)) + proj_bias
    normed_two = low(layer_norm(middle, norm2_gain, norm2_bias))
    active = low_back(project(normed_two, fc1_weight)) + fc1_bias
    hidden = low(jax.nn.gelu(active, approximate=False))
    result = middle + low_back(project(hidden, fc2_weight)) + fc2_bias
    return result * row_valid[..., None]

def reference(tokens, skip_feats, lengths, cotangent, skip_weight, skip_bias, norm1_gain, norm1_bias, qkv_weight, proj_weight, proj_bias, norm2_gain, norm2_bias, fc1_weight, fc1_bias, fc2_weight, fc2_bias):
    params = tuple((w.astype(jnp.float32) for w in (skip_weight, skip_bias, norm1_gain, norm1_bias, qkv_weight, proj_weight, proj_bias, norm2_gain, norm2_bias, fc1_weight, fc1_bias, fc2_weight, fc2_bias)))
    blocks = ITEMS // ITEMS_DEV
    block_shape = (blocks, ITEMS_DEV, SLOTS, D)
    token_blocks = tokens.astype(jnp.float32).reshape(block_shape)
    skip_blocks = skip_feats.astype(jnp.float32).reshape(block_shape)
    cot_blocks = cotangent.astype(jnp.float32).reshape(block_shape)
    slot_index = jnp.arange(SLOTS, dtype=jnp.int32)
    valid_all = (slot_index[None, :] < lengths[:, None].astype(jnp.int32)).astype(jnp.float32)
    valid_blocks = valid_all.reshape(blocks, ITEMS_DEV, SLOTS)

    def scan_step(totals, inputs):
        token_block, skip_block, valid_block, cot_block = inputs

        def runner(param_set, token_in, skip_in):
            return forward(param_set, token_in, skip_in, valid_block)
        result, pullback = jax.vjp(runner, params, token_block, skip_block)
        grad_params, grad_tokens, grad_skip = pullback(cot_block)
        totals = jax.tree.map(lambda left, right: left + right, totals, grad_params)
        return (totals, (result, grad_tokens, grad_skip))
    zero_grads = jax.tree.map(jnp.zeros_like, params)
    totals, outputs = lax.scan(scan_step, zero_grads, (token_blocks, skip_blocks, valid_blocks, cot_blocks))
    result, grad_tokens, grad_skip = outputs
    full_shape = (ITEMS, SLOTS, D)
    return (result.reshape(full_shape).astype(jnp.bfloat16), grad_tokens.reshape(full_shape).astype(jnp.bfloat16), grad_skip.reshape(full_shape).astype(jnp.bfloat16), totals[0], totals[1], totals[2], totals[3], totals[4], totals[5], totals[6], totals[7], totals[8], totals[9], totals[10], totals[11], totals[12])
```

```python
import functools
import types

import jax
import jax.numpy as jnp
from jax import lax
from jax.experimental import pallas as pl
from jax.experimental.pallas import tpu as pltpu
from jax.sharding import PartitionSpec as P

HEADS = 16
HEAD_DIM = 72
NORM_EPS = 1e-05
MASKED = -1e30
LANE = 128
TILE = 384
ROWS = 32
F32 = jnp.float32
B16 = jnp.bfloat16
MESH = pl.DeviceIdType.MESH
VMEM_BYTES = 64 * 1024 * 1024


def up(n, m):
    return -(-n // m) * m


def mm(a, b):
    return lax.dot_general(a, b, (((1,), (0,)), ((), ())), preferred_element_type=F32)


def mm_nt(a, b):
    return lax.dot_general(a, b, (((1,), (1,)), ((), ())), preferred_element_type=F32)


def mm_tn(a, b):
    return lax.dot_general(a, b, (((0,), (0,)), ((), ())), preferred_element_type=F32)


def iota(shape, dim):
    return lax.broadcasted_iota(jnp.int32, shape, dim)


def onehot(mask):
    return jnp.where(mask, 1.0, 0.0).astype(B16)


def rows_of(i, n=ROWS):
    return pl.ds(pl.multiple_of(i * n, n), n)


def lanes_of(i, n=TILE):
    return pl.ds(pl.multiple_of(i * n, LANE), n)


def loop(n, body, unroll=1, first=0):
    lax.fori_loop(first, first + n, lambda i, _: (body(i), None)[1], None, unroll=unroll)


def sizes(half, width, hidden_width, dp_count):
    z = types.SimpleNamespace()
    z.half, z.D, z.FF = half, width, hidden_width
    z.HP = up(half, 16)
    z.S = 2 * z.HP
    z.SP = up(z.S, LANE)
    z.FH = hidden_width // 2
    z.DH = width // 2
    z.WS = z.DH // LANE * LANE
    z.LO = z.DH - z.WS
    z.W = width - z.WS
    z.HN = HEADS // 2
    z.HS = z.HN // 2 * HEAD_DIM
    z.SW = z.HS // LANE * LANE
    z.SL = up(z.HS + z.LO + z.HS - z.SW, LANE)
    z.PQ = up(3 * z.HS, LANE)
    z.QN = dp_count // 2
    z.QH = z.QN // 2
    z.QP = z.QN // 4
    z.bits = z.QN.bit_length() - 1
    z.far = z.bits > 3
    z.NB = 2 * z.QN
    blocks = 4 * z.QN
    z.r2, z.rs, z.rp, z.r1 = hidden_width // blocks, 2 * width // blocks, width // blocks, width // z.QN
    z.r2p, z.rsp, z.rpp, z.r1p = (up(v, 16) for v in (z.r2, z.rs, z.rp, z.r1))
    return z


def transpose_block(src, block, r, rp, shift, sp, total):
    span = min(up(r + LANE - 1, LANE), total)
    first = shift + block * r
    start = jnp.minimum(first // LANE * LANE, total - span)
    start = pl.multiple_of(start, LANE)
    row, lane = iota((rp, span), 0), iota((rp, span), 1)
    pick = onehot((lane == row + (first - start)) & (row < r))
    return mm_nt(pick, src[0:sp, pl.ds(start, span)]).astype(B16)


def jobs_of(z):
    rest = list(range(2, z.bits))
    near, far = [0, 1, *rest], [1, 0, *rest]
    jobs, base = [], 0
    for name, group, r, rp, start, n, w, parts, order in (
        ("2a", "2", z.r2, z.r2p, 0, 2 * TILE, TILE, 1, near),
        ("2b", "2", z.r2, z.r2p, 2 * TILE, z.D - 2 * TILE, TILE, 1, far),
        ("1a", "1", z.r1, z.r1p, 0, 2 * TILE, TILE, 1, near),
        ("1b", "1", z.r1, z.r1p, 2 * TILE, z.FH // 2 - 2 * TILE, TILE, 1, far),
        ("p", "p", z.rp, z.rpp, 0, z.D, TILE, 1, far),
        ("qa", "q", z.r1, z.r1p, 0, 512, 512, 1, near),
        ("qb", "q", z.r1, z.r1p, 512, z.PQ - 512, TILE, 1, far),
        ("s", "s", z.rs, z.rsp, 0, z.D, TILE, 1, near),
    ):
        jobs.append(
            types.SimpleNamespace(
                name=name, group=group, r=r, rp=rp, start=start, n=n, w=w, nt=n // w, parts=parts, order=order, base=base
            )
        )
        base += n // w * parts
    return jobs, base


GROUPS = "21pqs"


def landing_of(z):
    return {
        f"rv{j.name}{s}": ((j.nt,) + (2,) * (z.bits - 1 - s) + (j.rp, j.w), z.far and s > 0)
        for j in jobs_of(z)[0]
        for s in range(z.bits)
    }


INS = (
    "lens", "tok", "sk", "cot", "sb", "g1", "h1", "pb", "g2", "h2", "b1", "b2", "sw", "qw", "pw", "f1", "f2",
)
LEFT_OUTS = ("LT2", "LT1", "LTq", "LTp", "LTs", "R1", "Rp", "Rq")


def any_outs(z):
    return LEFT_OUTS + tuple(n for n, (_, out) in landing_of(z).items() if out)


VMEM_OUTS = ("bo", "tg", "sg", "w2", "w1", "wp", "wq", "ws", "vout")


def out_shapes(z):
    s = jax.ShapeDtypeStruct
    landing = {n: s(shape, B16) for n, (shape, _) in landing_of(z).items()}
    left = lambda rows: s((2, 2, 2, z.QP, rows, z.SP), B16)
    return landing | dict(
        LT2=left(z.r2p),
        LT1=left(z.r1p),
        LTq=left(z.r1p),
        LTp=left(z.rpp),
        LTs=left(z.rsp),
        R1=s((2, z.S, z.FH // 2), B16),
        Rp=s((2, z.S, z.D), B16),
        Rq=s((2, z.S, z.PQ), B16),
        bo=s((z.half, z.D), B16),
        tg=s((z.half, z.D), B16),
        sg=s((2 * z.half, z.DH), B16),
        w2=s((z.r2, z.D), F32),
        w1=s((z.r1 // 4, z.FF), F32),
        wp=s((z.rp, z.D), F32),
        wq=s((z.r1 // 4, 3 * z.D), F32),
        ws=s((z.rs, z.D), F32),
        vout=s((16, z.D), F32),
    )


def scratch_of(z):
    v, dma = pltpu.VMEM, pltpu.SemaphoreType.DMA
    jobs, tiles = jobs_of(z)
    fp = up(z.r1 // 4, 8)
    out = dict(
        tokin=v((2, z.HP, z.D), B16),
        skin=v((2, z.S, z.W), B16),
        lent=v((2, 8, LANE), F32),
        dfin=v((2, z.S, z.D), B16),
        acc0=v((z.S, z.D), F32),
        acc1=v((z.S, z.D), F32),
        acc2=v((z.S, z.D), F32),
        acc3=v((z.HP, z.D), F32),
        psend=v((z.D // TILE, z.S, TILE), B16),
        pin0=v((z.D // TILE, z.S, TILE), B16),
        pin1=v((z.D // TILE, z.S, TILE), B16),
        pin3=v((z.HP, z.D), B16),
        pk=v((z.S, 3 * z.W), B16),
        probs=v((z.HN, z.S, z.S), B16),
        dact=v((z.S, z.FH), B16),
        dbase=v((2, z.S, z.D), B16),
        st2=v((4, 2, z.QP, z.r2p, z.SP), B16),
        st1=v((2, 2, z.QP, z.r1p, z.SP), B16),
        heads=v((z.SP, z.W), B16),
        bosum=v((z.HP, z.D), B16),
        rowv=v((8, z.D), F32),
        b1v=v((1, z.FF), F32),
        fbias=v((1, z.FH), F32),
        vb=v((3 + z.bits, 16, z.D), F32),
        vr=v((2 + z.bits, 16, z.D), F32),
    )
    for n, (shape, outside) in landing_of(z).items():
        if not outside:
            out[n] = v(shape, B16)
    for n, cols in (("1", z.FH // 2), ("q", z.PQ)):
        out["fr" + n] = v((4, fp, cols), F32)
    out["wsem"] = dma((12,))
    out["lsem"] = dma((16,))
    out["ssem"], out["rsem"] = dma((64,)), dma((64,))
    out["semld"] = dma((len(GROUPS), 6))
    out["semgs"], out["semgr"] = dma((z.bits, tiles)), dma((z.bits, tiles))
    out["semfs"], out["semfr"] = dma((2, 4)), dma((2, 4))
    out["semvs"], out["semvr"] = dma((2 + z.bits,)), dma((2 + z.bits,))
    return out


def scope_one(z):
    v = pltpu.VMEM
    return dict(
        qwv=v((z.D, 3 * z.W), B16),
        pwv=v((z.W, z.D), B16),
        f1v=v((z.D, z.FH), B16),
        f2v=v((z.FH, z.D), B16),
        atile=v((z.S, TILE), F32),
        hidden=v((z.SP, z.FH), B16),
        normed=v((z.SP, z.D), B16),
        normed2=v((z.SP, z.D), B16),
        stq=v((2, 2, z.QP, z.r1p, z.SP), B16),
        sts=v((4, 2, z.QP, z.rsp, z.SP), B16),
    )


def scope_start(z):
    v = pltpu.VMEM
    return dict(
        tokpad=v((z.HP, z.D), B16),
        skpad=v((z.S, z.W), B16),
        xin=v((z.SP, z.D), B16),
    )


def scope_two(z):
    v = pltpu.VMEM
    jobs, _ = jobs_of(z)
    out = dict(
        dmidl=v((z.S, z.D), B16),
        dpack=v((z.S, 3 * z.W), B16),
        slab=v((2, z.S, z.PQ), B16),
        stp=v((4, 2, z.QP, z.rpp, z.SP), B16),
        slotl=v((1, 2, 2, 2, z.QP, max(z.r1p, z.r2p, z.rsp), z.SP), B16),
        slotr=v((1, 2 * z.SP, z.D), B16),
    )
    if z.far:
        out["zin"] = v((z.QP, max(j.rp for j in jobs), 512), B16)
    for j in jobs:
        out["pr" + j.name] = v((j.nt,) + (2,) * z.bits + (j.rp, j.w), B16)
    return out


def scope_back(z):
    v = pltpu.VMEM
    return dict(qwb=v((z.D, 3 * z.W), B16), pwb=v((z.W, z.D), B16))


def scope_end(z):
    v = pltpu.VMEM
    fp = up(z.r1 // 4, 8)
    return dict(
        swb=v((z.D, z.D), B16),
        sumt=v((z.r1p, 512), F32),
        fs1=v((4, fp, z.FH // 2), F32),
        fsq=v((4, fp, z.PQ), F32),
    )


def kernel(z, *refs):
    scratch = scratch_of(z)
    r = types.SimpleNamespace(**dict(zip((*INS, *any_outs(z), *VMEM_OUTS, *scratch), refs, strict=True)))
    jobs, _ = jobs_of(z)
    j2a, j2b, j1a, j1b, jp, jqa, jqb, js = jobs
    d, x = lax.axis_index("dp"), lax.axis_index("seq")
    c, q = lax.rem(d, 2), d // 2
    bit = [lax.rem(q // 2**b, 2) for b in range(z.bits)]
    me = 2 * c + x
    peer, xpeer = (d + 1 - 2 * c, x), (d, 1 - x)
    across = [(d + (1 - 2 * bit[b]) * 2 ** (b + 1), x) for b in range(z.bits)]
    D, S, HP, half = z.D, z.S, z.HP, z.half
    nt = D // TILE

    def scoped(spec, body):
        def inner(*held):
            for name, ref in zip(spec, held, strict=True):
                setattr(r, name, ref)
            body()
            for name in spec:
                delattr(r, name)

        pl.run_scoped(inner, *spec.values())

    def quad(k):
        return (2 * q + k // 2, lax.rem(k, 2))

    def copy_to(src, dst, ss, rs, dev):
        return pltpu.make_async_remote_copy(
            src_ref=src, dst_ref=dst, send_sem=ss, recv_sem=rs, device_id=dev, device_id_type=MESH
        )

    used = [0]

    def slots(n):
        used[0] += n
        return used[0] - n

    def remote(src, dst, slot, dev):
        return copy_to(src, dst, r.ssem.at[slot], r.rsem.at[slot], dev)

    def wait_recv(dst, slot):
        remote(dst, dst, slot, xpeer).wait_recv()

    def wait_send(src, slot):
        remote(src, src, slot, xpeer).wait_send()

    def local(src, dst, n):
        return pltpu.make_async_copy(src, dst, r.lsem.at[n])

    def load(src, dst, n):
        return pltpu.make_async_copy(src, dst, r.wsem.at[n])

    def at16(start, n):
        return pl.ds(pl.multiple_of(start, 16), n)

    def at128(start, n):
        return pl.ds(pl.multiple_of(start, LANE), n)

    hx, hx1, hc, hc1 = (at16(HP * v, HP) for v in (x, 1 - x, c, 1 - c))

    S_LEN, S_TOK, S_SK, S_COT, S_P0, S_P1, S_P2, S_P4 = (slots(n) for n in (1, 2, 2, 3, nt, nt, nt, nt))
    S_P3, S_TS, S_TP, S_T2, S_XQ, S_X1, S_XP, S_XS, S_R1, S_RQ, S_BO = (
        slots(n) for n in (1, 3, 3, 6, 2, 2, 2, 2, 1, 1, 1)
    )

    barrier = pltpu.get_barrier_semaphore()
    for t in range(1, 4):
        pl.semaphore_signal(barrier, inc=1, device_id=quad(lax.rem(me + t, 4)), device_id_type=MESH)
    for other in across:
        pl.semaphore_signal(barrier, inc=1, device_id=other, device_id_type=MESH)
    pl.semaphore_wait(barrier, 3 + z.bits)

    def qkv_loads(dst):
        return [
            load(r.qw.at[:, at128(D * j + z.WS * c, z.W)], dst.at[:, z.W * j : z.W * (j + 1)], 1 + j) for j in range(3)
        ]

    def proj_load(dst):
        return load(r.pw.at[at16(z.WS * c, z.W), :], dst, 4)

    def partial_sums(value, mine, theirs, slot):
        def step(i):
            v = value(i)
            at = lanes_of(i)
            mine[:, at] = v
            r.psend[i] = v.astype(B16)
            remote(r.psend.at[i], theirs.at[i], slot + i, peer).start()

        loop(nt, step)

    def partial_done(theirs, slot):
        def step(i):
            remote(r.psend.at[i], theirs.at[i], slot + i, peer).wait()

        loop(nt, step)

    def spread_blocks(src, stage, rr, rrp, shift, out, slot, lslot, part=0, parts=1):
        n = z.NB // parts
        known = src.shape[1] * (part + 1) // parts

        def step(b):
            m = b // 4
            stage[lax.rem(b, 4), m // z.QP, lax.rem(m, z.QP)] = transpose_block(src, b, rr, rrp, shift, z.SP, known)

        loop(n, step, 4, part * n)
        some = slice(part, part + 1) if parts > 1 else slice(0, 2)
        for t in range(1, 4):
            k = lax.rem(me + t, 4)
            remote(stage.at[k, some], out.at[x, c, some], slot + part * 3 + t - 1, quad(k)).start()
        local(stage.at[me, some], out.at[x, c, some], lslot + part).start(priority=1)

    def spread_sent(stage, out, slot, lslot, parts=1):
        n = 2 // parts
        for i in range(3 * parts):
            wait_send(stage.at[0, 0:n], slot + i)
        for part in range(parts):
            local(stage.at[0, 0:n], out.at[x, 0, 0:n], lslot + part).wait()

    def spread_here(out, slot, part=0, parts=1):
        for i in range(3):
            wait_recv(out.at[x, 0, 0 : 2 // parts], slot + part * 3 + i)

    def whole_blocks(src, stage, out, slot, lslot):
        def step(b):
            stage[b // (2 * z.QP), lax.rem(b // z.QP, 2), lax.rem(b, z.QP)] = transpose_block(
                src, b, z.r1, z.r1p, 0, z.SP, D
            )

        loop(z.QN, step, 4)
        remote(stage.at[c], out.at[x, c], slot, xpeer).start()
        local(stage, out.at[x], lslot).start(priority=1)

    def relay(out, part, slot):
        wait_recv(out.at[1 - x, part], slot)
        remote(out.at[1 - x, part], out.at[1 - x, part], slot + 1, peer).start()

    def whole(tiles, at):
        return jnp.concatenate([tiles[t, at] for t in range(nt)], axis=1).astype(F32)

    def normalise(v, gain, shift):
        mean = jnp.mean(v, axis=-1, keepdims=True)
        centred = v - mean
        var = jnp.mean(centred * centred, axis=-1, keepdims=True)
        return centred * lax.rsqrt(var + NORM_EPS) * gain + shift

    def norm_back(v, dn, gain):
        mean = jnp.mean(v, axis=-1, keepdims=True)
        centred = v - mean
        var = jnp.mean(centred * centred, axis=-1, keepdims=True)
        rstd = lax.rsqrt(var + NORM_EPS)
        hat = centred * rstd
        dh = dn * gain
        one = jnp.mean(dh, axis=-1, keepdims=True)
        two = jnp.mean(dh * hat, axis=-1, keepdims=True)
        return rstd * (dh - one - hat * two), dn * hat

    def fold(v):
        return jnp.sum(v, axis=0, keepdims=True)

    zero = jnp.zeros((1, D), F32)
    SB, G1, H1, PB, G2, H2, B2 = range(7)

    def rowp(i):
        return r.rowv[i : i + 1, :]

    tok_self, sk_self = (c == 0) & (x == 0), (c == 1) & (x == 1)
    span = 2 * LANE
    scale = HEAD_DIM ** (-0.5)

    def head_window(h):
        first = z.LO * c + HEAD_DIM * h
        start = pl.multiple_of(jnp.minimum(first // LANE * LANE, z.W - span), LANE)
        lane = iota((1, span), 1) + start
        keep = jnp.where((lane >= first) & (lane < first + HEAD_DIM), 1.0, 0.0)
        return start, keep

    def length_here():
        return jnp.where(c == x, r.lent[0], r.lent[1])[0:1, 0:1]

    def begin():
        load(r.sw.at[at16(D * c, D)], r.f1v.at[:, 0:D], 0).start(priority=1)
        for v in qkv_loads(r.qwv):
            v.start(priority=1)
        proj_load(r.pwv).start(priority=1)
        length = r.lens[0].astype(F32)
        r.lent[0] = jnp.full((8, LANE), length, F32)
        remote(r.lent.at[0], r.lent.at[1], S_LEN, peer).start()
        spread = onehot((iota((HP, half), 0) == iota((HP, half), 1)))
        r.tokpad[...] = mm(spread, r.tok[...]).astype(B16)

        @pl.when(tok_self)
        def _():
            r.tokin[x] = r.tokpad[...]

        @pl.when(jnp.logical_not(tok_self))
        def _():
            remote(r.tokpad, r.tokin.at[x], S_TOK + x, quad(c)).start()

        row, col = iota((S, 2 * half), 0), iota((S, 2 * half), 1)
        pick = onehot(((row < half) & (row == col)) | ((row >= HP) & (row < HP + half) & (col == row - (HP - half))))
        shift = onehot(iota((z.DH, z.W), 1) == iota((z.DH, z.W), 0) + z.LO * x)
        r.skpad[...] = mm(mm(pick, r.sk[...]).astype(B16), shift).astype(B16)

        @pl.when(sk_self)
        def _():
            r.skin[x] = r.skpad[...]

        @pl.when(jnp.logical_not(sk_self))
        def _():
            remote(r.skpad, r.skin.at[x], S_SK + x, quad(2 + c)).start()

        own_row = iota((HP, 1), 0)
        live = (own_row < half) & ((own_row + half * x).astype(F32) < length)
        r.dfin[c, hx] = jnp.where(live, mm(spread, r.cot[...]), 0.0).astype(B16)

        for ref in (r.xin, r.normed, r.normed2, r.hidden):
            ref[S:, :] = jnp.zeros((z.SP - S, ref.shape[1]), B16)
        r.heads[...] = jnp.zeros(r.heads.shape, B16)
        for i, ref in enumerate((r.sb, r.g1, r.h1, r.pb, r.g2, r.h2, r.b2)):
            r.rowv[i : i + 1, :] = ref[...].astype(F32).reshape(1, D)
        r.b1v[...] = r.b1[...].astype(F32).reshape(1, z.FF)

        for h in range(2):
            @pl.when((c == 0) & jnp.logical_not(tok_self & (h == 0)))
            def _(h=h):
                wait_recv(r.tokin.at[h], S_TOK + h)

            @pl.when((c == 1) & jnp.logical_not(sk_self & (h == 1)))
            def _(h=h):
                wait_recv(r.skin.at[h], S_SK + h)

        remote(r.dfin.at[c, hx], r.dfin.at[c, hx], S_COT, xpeer).start()
        remote(r.dfin.at[c, hx], r.dfin.at[c, hx], S_COT + 1, peer).start()

        @pl.when(c == 0)
        def _():
            for h in range(2):
                r.xin[h * HP : (h + 1) * HP, :] = r.tokin[h]

        @pl.when(c == 1)
        def _():
            r.xin[0:S, 0 : z.WS] = r.skin[0, :, 0 : z.WS]
            r.xin[0:S, z.WS : z.W] = r.skin[0, :, z.WS : z.W] + r.skin[1, :, 0 : z.W - z.WS]
            r.xin[0:S, z.W : D] = r.skin[1, :, z.W - z.WS : z.W]

        load(r.sw.at[at16(D * c, D)], r.f1v.at[:, 0:D], 0).wait()
        partial_sums(lambda i: mm(r.xin[0:S], r.f1v[:, lanes_of(i)]), r.acc0, r.pin0, S_P0)
        spread_blocks(r.xin, r.sts, z.rs, z.rsp, 0, r.LTs, S_TS, 0)

        @pl.when(jnp.logical_not(tok_self))
        def _():
            wait_send(r.tokpad, S_TOK + x)

        @pl.when(jnp.logical_not(sk_self))
        def _():
            wait_send(r.skpad, S_SK + x)

    def ff_loads():
        return [load(r.f1.at[:, at128(z.FH * c, z.FH)], r.f1v, 5), load(r.f2.at[at16(z.FH * c, z.FH), :], r.f2v, 6)]

    def forward():
        scoped(scope_start(z), begin)
        for v in ff_loads():
            v.start(priority=1)
        partial_done(r.pin0, S_P0)

        def norm_one(i):
            at = rows_of(i)
            v = r.acc0[at] + whole(r.pin0, at) + rowp(SB)
            r.acc0[at] = v
            r.normed[at] = normalise(v, rowp(G1), rowp(H1)).astype(B16)

        loop(S // ROWS, norm_one, S // ROWS)
        for v in qkv_loads(r.qwv):
            v.wait()

        def qkv_tile(i):
            r.pk[:, lanes_of(i)] = mm(r.normed[0:S], r.qwv[:, lanes_of(i)]).astype(B16)

        loop(3 * z.W // TILE, qkv_tile)

        wait_recv(r.dfin.at[c, hx1], S_COT)
        remote(r.dfin.at[c, hx1], r.dfin.at[c, hx1], S_COT + 2, peer).start()

        wait_recv(r.lent.at[1], S_LEN)
        slot_col = iota((1, S), 1)
        slot_of = jnp.where(slot_col < HP, slot_col, slot_col - (HP - half))
        key_ok = ((slot_col < half) | ((slot_col >= HP) & (slot_col < HP + half))) & (
            slot_of.astype(F32) < length_here()
        )

        def head_forward(h):
            start, keep = head_window(h)
            query = r.pk[:, pl.ds(start, span)] * keep.astype(B16)
            key = r.pk[:, at128(z.W + start, span)]
            value = r.pk[:, at128(2 * z.W + start, span)]
            scores = jnp.where(key_ok, mm_nt(query, key) * scale, MASKED)
            top = jnp.max(scores, axis=-1, keepdims=True)
            e = jnp.exp(scores - top)
            probs = (e * (1.0 / jnp.sum(e, axis=-1, keepdims=True))).astype(B16)
            r.probs[h] = probs
            at = pl.ds(start, span)
            r.heads[0:S, at] = r.heads[0:S, at] + (mm(probs, value) * keep).astype(B16)

        loop(z.HN, head_forward, 2)

        proj_load(r.pwv).wait()
        partial_sums(lambda i: mm(r.heads[0:S], r.pwv[:, lanes_of(i)]), r.acc1, r.pin1, S_P1)
        whole_blocks(r.normed, r.stq, r.LTq, S_XQ, 1)
        partial_done(r.pin1, S_P1)

        def norm_two(i):
            at = rows_of(i)
            v = r.acc0[at] + r.acc1[at] + whole(r.pin1, at) + rowp(PB)
            r.acc1[at] = v
            r.normed2[at] = normalise(v, rowp(G2), rowp(H2)).astype(B16)

        loop(S // ROWS, norm_two, S // ROWS)

        whole_blocks(r.normed2, r.st1, r.LT1, S_X1, 4)
        wait_recv(r.dfin.at[1 - c, hx], S_COT + 1)
        wait_recv(r.dfin.at[1 - c, hx1], S_COT + 2)
        for v in ff_loads():
            v.wait()

        def hidden_tile(i):
            at = lanes_of(i)
            a = mm(r.normed2[0:S], r.f1v[:, at]) + r.b1v[:, at128(z.FH * c + i * TILE, TILE)]
            dh = mm_nt(r.dfin[x], r.f2v[rows_of(i, TILE), :])
            cdf = 0.5 * (1.0 + lax.erf(a * (2.0**-0.5)))
            pdf = jnp.exp(-0.5 * a * a) * (0.5 / jnp.pi) ** 0.5
            r.hidden[0:S, at] = (a * cdf).astype(B16)
            da = dh * (cdf + a * pdf)
            r.dact[:, at] = da.astype(B16)
            r.fbias[:, at] = fold(da)

        tiles, fq = z.FH // TILE // 2, z.FH // 2
        loop(tiles, lambda i: hidden_tile(tiles * (1 - x) + i), tiles)
        remote(r.dact.at[:, at128(fq * (1 - x), fq)], r.R1.at[x], S_R1, xpeer).start()
        relay(r.LTq, c, S_XQ)
        relay(r.LT1, c, S_X1)
        loop(tiles, lambda i: hidden_tile(tiles * x + i), tiles)
        partial_sums(lambda i: mm_nt(r.dact[...], r.f1v[rows_of(i, TILE), :]), r.acc2, r.pin0, S_P2)
        spread_blocks(r.hidden, r.st2, z.r2, z.r2p, 0, r.LT2, S_T2, 8)
        local(r.dact.at[:, at128(fq * x, fq)], r.R1.at[x], 3).start(priority=1)

        def result_tile(i):
            at = lanes_of(i)
            r.atile[...] = mm(r.hidden[0:S], r.f2v[:, at])
            r.acc3[:, at] = r.atile[hc]
            r.tokin[0, :, at] = r.atile[hc1].astype(B16)

        loop(nt, result_tile)
        remote(r.tokin.at[0], r.pin3, S_P3, peer).start()
        spread_sent(r.sts, r.LTs, S_TS, 0)
        wait_send(r.stq.at[c], S_XQ)
        local(r.stq, r.LTq.at[x], 1).wait()

    def ref(kind, j):
        return getattr(r, kind + j.name)

    def tile(j, i):
        return at128(j.start + i * j.w, j.w)

    def group_loads(j, part):
        n = GROUPS.index(j.group)
        s = n % r.slotl.shape[0]
        left = getattr(r, "LT" + j.group)
        right = {"2": r.dfin, "1": r.R1, "p": r.Rp, "q": r.Rq, "s": r.dbase}[j.group]
        some = slice(0, 2) if part is None else slice(part, part + 1)
        for i in range(2):
            yield pltpu.make_async_copy(
                left.at[i, :, some], r.slotl.at[s, i, :, some, :, 0 : j.rp], r.semld.at[n, 2 * (part or 0) + i]
            )
            if not part:
                yield pltpu.make_async_copy(
                    right.at[i], r.slotr.at[s, i * z.SP : i * z.SP + S, 0 : right.shape[-1]], r.semld.at[n, 4 + i]
                )

    def kept(j, s, keep, part=None):
        at = [slice(None)] * z.bits
        for b in j.order[:s]:
            at[z.bits - 1 - b] = bit[b]
        b = j.order[s]
        at[z.bits - 1 - b] = bit[b] if keep else 1 - bit[b]
        if part is not None:
            at[1] = slice(part, part + 1)
        return tuple(at)

    def landed(j, s):
        return getattr(r, f"rv{j.name}{s}")

    def half_copy(j, s, i, part=0):
        split = s == 0 and j.parts > 1
        src = ref("pr", j).at[(i, *kept(j, s, False, part if split else None))]
        dst = landed(j, s)
        lead = (i, slice(None), slice(part, part + 1)) if split else (i,)
        n = j.base + part * j.nt + i
        return copy_to(src, dst.at[lead], r.semgs.at[s, n], r.semgr.at[s, n], across[j.order[s]])

    def prep(j, part=None):
        for v in group_loads(j, part):
            v.start(priority=1)

    def ready(j, part=None):
        for v in group_loads(j, part):
            v.wait()

    def products(j, part=0):
        s = GROUPS.index(j.group) % r.slotl.shape[0]

        def step(i):
            at = tile(j, i)
            if j.parts > 1:
                left = [r.slotl[s, n, :, part, :, 0 : j.rp] for n in range(2)]
                to = (slice(None), part)
            else:
                left = [r.slotl[s, n, :, :, :, 0 : j.rp] for n in range(2)]
                to = ()
            left = [v.reshape(z.QN // j.parts * j.rp, z.SP) for v in left]
            out = mm(jnp.concatenate(left, axis=1), r.slotr[s, :, at])
            shape = (2,) * (z.bits - (j.parts > 1)) + (j.rp, j.w)
            ref("pr", j)[(i, *to)] = out.astype(B16).reshape(shape)
            half_copy(j, 0, i, part).start()

        loop(j.nt, step)

    def sums(j, s, store=None):
        def step(i):
            at = tile(j, i)
            for part in range(j.parts if s == 0 else 1):
                half_copy(j, s, i, part).wait_recv()
            here = (i, *kept(j, s, True))
            theirs = landed(j, s)
            if z.far and s > 0:
                n = 2 ** (z.bits - 1 - s)
                stage = r.zin.at[0:n, 0 : j.rp, 0 : j.w]
                for k in range(n):
                    pick = tuple(k // 2**b % 2 for b in reversed(range(z.bits - 1 - s)))
                    fetch = local(theirs.at[(i, *pick)], stage.at[k], 15)
                    fetch.start()
                    fetch.wait()
                piece = stage[...].reshape(theirs.shape[1:])
            else:
                piece = theirs[i]
            total = ref("pr", j)[here].astype(F32) + piece.astype(F32)
            if s < z.bits - 1:
                ref("pr", j)[here] = total.astype(B16)
                half_copy(j, s + 1, i).start()
            else:
                store(at, total)

        loop(j.nt, step)

    def more_sums(j):
        for s in range(2, z.bits - 1):
            sums(j, s)

    def sums_sent(j):
        def step(i):
            for s in range(z.bits):
                for part in range(j.parts if s == 0 else 1):
                    half_copy(j, s, i, part).wait_send()

        loop(j.nt, step)

    rq = z.r1 // 4

    def fix_copy(n, g, t):
        k = lax.rem(me + t, 4)
        src, dst = getattr(r, "fs" + g), getattr(r, "fr" + g)
        return copy_to(src.at[k], dst.at[me], r.semfs.at[n, t - 1], r.semfr.at[n, t - 1], quad(k))

    def fix_start(n, g):
        for t in range(1, 4):
            fix_copy(n, g, t).start()
        getattr(r, "fr" + g)[me] = getattr(r, "fs" + g)[me]

    def fix_wait(n, g):
        for t in range(1, 4):
            fix_copy(n, g, t).wait()

    def direct(out):
        def store(at, total):
            out[:, at] = total[0 : out.shape[0]]

        return store

    def summed(out):
        def store(at, total):
            w = total.shape[1]
            r.sumt[:, 0:w] = total
            for k in range(4):
                out[k, 0:rq, at] = r.sumt[k * rq : (k + 1) * rq, 0:w]

        return store

    v_devs = (peer, xpeer, *across)

    def v_copy(s):
        return copy_to(r.vb.at[s], r.vr.at[s], r.semvs.at[s], r.semvr.at[s], v_devs[s])

    def v_step(s):
        if s > 0:
            v_copy(s - 1).wait()
            r.vb[s] = r.vb[s - 1] + r.vr[s - 1]
        if s < len(v_devs):
            v_copy(s).start()

    def back():
        for v in qkv_loads(r.qwb):
            v.start(priority=1)
        proj_load(r.pwb).start(priority=1)
        for s in range(r.slotr.shape[0]):
            for i in range(2):
                r.slotr[s, i * z.SP + S : (i + 1) * z.SP, :] = jnp.zeros((z.SP - S, D), B16)
        r.dpack[...] = jnp.zeros(r.dpack.shape, B16)
        partial_done(r.pin0, S_P2)

        def norm_two_back(i, sums):
            at = rows_of(i)
            dn = r.acc2[at] + whole(r.pin0, at)
            dv, dg = norm_back(r.acc1[at], dn, rowp(G2))
            df = r.dfin[x, at].astype(F32)
            dm = df + dv
            r.acc2[at] = dm
            r.dmidl[at] = dm.astype(B16)
            return sums[0] + fold(dg), sums[1] + fold(dn), sums[2] + fold(df), sums[3] + fold(dm)

        dg2, dh2, db2, dpb = lax.fori_loop(0, S // ROWS, norm_two_back, (zero, zero, zero, zero))
        local(r.dmidl, r.Rp.at[x], 6).start(priority=1)
        wait_recv(r.LT1.at[1 - x, 1 - c], S_X1 + 1)
        local(r.st1, r.LT1.at[x], 4).wait()
        wait_recv(r.R1.at[1 - x], S_R1)
        local(r.R1.at[x], r.R1.at[x], 3).wait()
        prep(j1a)
        r.vb[0] = jnp.zeros((16, D), F32)
        first = jnp.where(c == 0, 1.0, 0.0)
        for i, v in ((3, dpb), (4, dg2), (5, dh2), (6, db2)):
            r.vb[0, i : i + 1, :] = v * first
        for j in range(z.FH // D):
            v = r.fbias[:, j * D : (j + 1) * D]
            r.vb[0, 8 + j : 9 + j, :] = v * first
            r.vb[0, 10 + j : 11 + j, :] = v * (1.0 - first)

        proj_load(r.pwb).wait()
        r.skin[0] = mm_nt(r.dmidl[...], r.pwb[...]).astype(B16)
        ready(j1a)
        products(j1a)
        products(j1b)

        def head_backward(h):
            start, keep = head_window(h)
            low = keep.astype(B16)
            at_q, at_k, at_v = pl.ds(start, span), at128(z.W + start, span), at128(2 * z.W + start, span)
            query, key, value = r.pk[:, at_q], r.pk[:, at_k], r.pk[:, at_v]
            dh = r.skin[0, :, at_q]
            probs = r.probs[h]
            dp = mm_nt(dh * low, value)
            pf = probs.astype(F32)
            delta = jnp.sum(dp * pf, axis=-1, keepdims=True)
            ds = (pf * (dp - delta) * scale).astype(B16)
            r.dpack[:, at_q] = r.dpack[:, at_q] + (mm(ds, key) * keep).astype(B16)
            r.dpack[:, at_k] = r.dpack[:, at_k] + (mm_tn(ds, query) * keep).astype(B16)
            r.dpack[:, at_v] = r.dpack[:, at_v] + (mm_tn(probs, dh) * keep).astype(B16)

        def slab_of(mine, part):
            first = z.LO * c + (z.HS - z.SW) * part
            row, lane = iota((z.SL, z.SL), 0), iota((z.SL, z.SL), 1)
            out = []
            for t in range(3):
                to = z.HS * t // LANE * LANE
                move = onehot((row - first == lane - (z.HS * t - to)) & (row >= first) & (row < first + z.HS))
                out.append((to, mm(r.dpack[:, at128(z.W * t + z.SW * part, z.SL)], move).astype(B16)))
            for at in range(0, z.PQ, LANE):
                held = [v[:, at - to : at - to + LANE] for to, v in out if to <= at < to + z.SL]
                r.slab[mine, :, at : at + LANE] = held[0] if len(held) == 1 else held[0] + held[1]

        nh = z.HN // 2
        loop(nh, lambda i: head_backward(nh * (1 - x) + i), 2)
        slab_of(0, 1 - x)
        remote(r.slab.at[0], r.Rq.at[x], S_RQ, xpeer).start()
        remote(r.dmidl.at[hc], r.Rp.at[x, hc], S_XP, xpeer).start()
        block_out()
        spread_here(r.LT2, S_T2)
        local(r.st2.at[0], r.LT2.at[x, 0], 8).wait()
        prep(j2a)
        ready(j2a)
        products(j2a)
        products(j2b)
        loop(nh, lambda i: head_backward(nh * x + i), 2)
        for v in qkv_loads(r.qwb):
            v.wait()
        partial_sums(lambda i: mm_nt(r.dpack[...], r.qwb[rows_of(i, TILE), :]), r.acc1, r.pin1, S_P4)
        slab_of(1, x)
        local(r.slab.at[1], r.Rq.at[x], 7).start(priority=1)
        spread_blocks(r.heads, r.stp, z.rp, z.rpp, z.LO * c, r.LTp, S_TP, 2)
        sums(j1a, 0)
        sums(j1b, 0)
        relay(r.Rp, hc, S_XP)

    def block_out():
        wait_recv(r.pin3, S_P3)
        slot_row = iota((HP, 1), 0)
        out_ok = (slot_row < half) & ((slot_row + half * c).astype(F32) < length_here())
        total = r.acc1[hc] + r.acc3[...] + r.pin3[...].astype(F32) + rowp(B2)
        r.tokin[1] = jnp.where(out_ok, total, 0.0).astype(B16)

        @pl.when(c == x)
        def _():
            r.bosum[...] = r.tokin[1]

    def finish():
        weight = [
            load(r.sw.at[0:D], r.swb, 8),
            load(r.sw.at[at16(D + z.DH * x, z.DH)], r.swb.at[0 : z.DH], 9),
        ]
        weight[0].start(priority=1)
        partial_done(r.pin1, S_P4)

        def norm_one_back(i, sums):
            at = rows_of(i)
            dn = r.acc1[at] + whole(r.pin1, at)
            dv, dg = norm_back(r.acc0[at], dn, rowp(G1))
            db = r.acc2[at] + dv
            r.dbase[x, at] = db.astype(B16)
            return sums[0] + fold(dg), sums[1] + fold(dn), sums[2] + fold(db)

        dg1, dh1, dsb = lax.fori_loop(0, S // ROWS, norm_one_back, (zero, zero, zero))
        first = jnp.where(c == 0, 1.0, 0.0)
        for i, v in enumerate((dsb, dg1, dh1)):
            r.vb[0, i : i + 1, :] = v * first
        v_step(0)

        remote(r.dbase.at[x, hc], r.dbase.at[x, hc], S_XS, xpeer).start()
        wait_recv(r.LTq.at[1 - x, 1 - c], S_XQ + 1)
        wait_recv(r.Rq.at[1 - x], S_RQ)
        local(r.Rq.at[x], r.Rq.at[x], 7).wait()
        prep(jqa)
        ready(jqa)
        products(jqa)
        products(jqb)
        wait_recv(r.Rp.at[1 - x, hc1], S_XP + 1)
        local(r.dmidl, r.Rp.at[x], 6).wait()
        spread_here(r.LTp, S_TP)
        spread_sent(r.stp, r.LTp, S_TP, 2)
        prep(jp)
        v_step(1)
        sums(j2b, 0)
        sums(j1b, 1)
        ready(jp)
        products(jp)
        sums(j1a, 1)
        relay(r.dbase, hc, S_XS)
        spread_here(r.LTs, S_TS)
        sums(j2a, 0)
        wait_recv(r.dbase.at[1 - x, hc1], S_XS + 1)
        prep(js)
        v_step(2)

        @pl.when(c != x)
        def _():
            remote(r.tokin.at[1], r.bosum, S_BO, (2 * q + x, c)).start()

        ready(js)
        products(js)
        more_sums(j1a)
        more_sums(j1b)
        v_step(3)
        sums(j2b, 1)
        sums(jp, 0)
        sums(jqb, 0)
        sums(j1b, z.bits - 1, summed(r.fs1))
        weight[0].wait()
        r.tg[...] = mm_nt(r.dbase[c, hx], r.swb[...]).astype(B16)[0:half]
        weight[1].start(priority=1)
        v_step(4)
        sums(j1a, z.bits - 1, summed(r.fs1))
        fix_start(0, "1")
        sums(j2a, 1)
        sums(jqa, 0)
        more_sums(j2a)
        more_sums(j2b)
        sums(j2b, z.bits - 1, direct(r.w2))
        weight[1].wait()
        sg = mm_nt(r.dbase[c], r.swb[0 : z.DH, :]).astype(B16)
        row, col = iota((2 * half, S), 0), iota((2 * half, S), 1)
        back_rows = onehot(((row < half) & (row == col)) | ((row >= half) & (col == row + (HP - half))))
        r.sg[...] = mm(back_rows, sg).astype(B16)
        for s in range(5, len(v_devs) + 1):
            v_step(s)
        r.vout[...] = r.vb[len(v_devs)]
        sums(jqb, 1)
        more_sums(jqb)
        sums(jp, 1)
        more_sums(jp)
        sums(js, 0)
        sums(j2a, z.bits - 1, direct(r.w2))

        @pl.when(c == x)
        def _():
            r.bosum[...] = r.tokin[1]

        @pl.when(c != x)
        def _():
            remote(r.tokin.at[1], r.bosum, S_BO, (2 * q + x, c)).wait()

        r.bo[...] = r.bosum[0:half]
        sums(jqa, 1)
        more_sums(jqa)
        sums(jqb, z.bits - 1, summed(r.fsq))
        fix_wait(0, "1")
        for k in range(4):
            r.w1[:, k * (z.FH // 2) : (k + 1) * (z.FH // 2)] = r.fr1[k, 0:rq]
        sums(jp, z.bits - 1, direct(r.wp))
        sums(js, 1)
        more_sums(js)
        sums(jqa, z.bits - 1, summed(r.fsq))
        fix_start(1, "q")
        sums(js, z.bits - 1, direct(r.ws))
        fix_wait(1, "q")
        for t in range(3):
            r.wq[:, t * D : (t + 1) * D] = jnp.concatenate(
                [r.frq[k, 0:rq, t * z.HS : (t + 1) * z.HS] for k in range(4)], axis=1
            )

        wait_send(r.lent.at[0], S_LEN)
        for j in range(3):
            wait_send(r.dfin.at[c, hx], S_COT + j)
        for j in range(3):
            wait_send(r.st2.at[0], S_T2 + j)
        wait_send(r.tokin.at[0], S_P3)
        wait_send(r.st1.at[c], S_X1)
        wait_send(r.dmidl.at[hc], S_XP)
        wait_send(r.dbase.at[x, hc], S_XS)
        wait_send(r.LTq.at[1 - x, c], S_XQ + 1)
        wait_send(r.LT1.at[1 - x, c], S_X1 + 1)
        wait_send(r.Rp.at[1 - x, hc], S_XP + 1)
        wait_send(r.dbase.at[1 - x, hc], S_XS + 1)
        wait_send(r.R1.at[x], S_R1)
        wait_send(r.slab.at[0], S_RQ)
        for j in jobs:
            sums_sent(j)

    def backward():
        scoped(scope_back(z), back)
        scoped(scope_end(z), finish)

    scoped(scope_one(z), forward)
    scoped(scope_two(z), backward)


def call(z, *args):
    outs = out_shapes(z)
    anywhere, vmem = pl.BlockSpec(memory_space=pl.ANY), pl.BlockSpec(memory_space=pltpu.VMEM)
    names = (*any_outs(z), *VMEM_OUTS)
    res = pl.pallas_call(
        functools.partial(kernel, z),
        out_shape=[outs[n] for n in names],
        in_specs=[pl.BlockSpec(memory_space=pltpu.SMEM), *([vmem] * 11), *([anywhere] * 5)],
        out_specs=[anywhere] * len(any_outs(z)) + [vmem] * len(VMEM_OUTS),
        scratch_shapes=list(scratch_of(z).values()),
        compiler_params=pltpu.CompilerParams(
            collective_id=0, has_side_effects=True, vmem_limit_bytes=VMEM_BYTES
        ),
        name="block",
    )(*args)
    return dict(zip(names, res))


def shards(tokens, skip_feats, lengths, cotangent, skip_weight, skip_bias, norm1_gain, norm1_bias, qkv_weight,
           proj_weight, proj_bias, norm2_gain, norm2_bias, fc1_weight, fc1_bias, fc2_weight, fc2_bias):
    dp_count = lax.axis_size("dp")
    half, width = tokens.shape[1:]
    z = sizes(half, width, fc1_weight.shape[1], dp_count)
    g = call(z, lengths, tokens[0], skip_feats[0], cotangent[0], skip_bias, norm1_gain, norm1_bias, proj_bias,
             norm2_gain, norm2_bias, fc1_bias, fc2_bias, skip_weight, qkv_weight, proj_weight, fc1_weight, fc2_weight)
    vec = g["vout"]
    b = 2 * lax.axis_index("dp") + lax.axis_index("seq")
    own = lax.dynamic_slice(vec, (0, b * z.rp), (8, z.rp))
    fb = lax.dynamic_slice(vec[8 : 8 + z.FF // width].reshape(-1), (b * z.r2,), (z.r2,))
    return (g["bo"][None], g["tg"][None], g["sg"][None], g["ws"], own[0], own[1], own[2], g["wq"], g["wp"], own[3],
            own[4], own[5], g["w1"], fb, g["w2"], own[6])


def solution(mesh):
    placed = (P("dp", "seq", None), P("dp", None, "seq"), P("dp"), P("dp", "seq", None), *([P()] * 13))
    both = ("dp", "seq")
    return jax.shard_map(
        shards, mesh=mesh, in_specs=placed,
        out_specs=(P("dp", "seq", None), P("dp", "seq", None), P("dp", None, "seq"), P(both, None), P(both), P(both),
                   P(both), P(both, None), P(both, None), P(both), P(both), P(both), P(both, None), P(both),
                   P(both, None), P(both)),
        check_vma=False,
    )
```

```python
import functools
import types

import jax
import jax.numpy as jnp
from jax import lax
from jax.experimental import pallas as pl
from jax.experimental.pallas import tpu as pltpu
from jax.sharding import PartitionSpec as P

HEADS = 16
HEAD_DIM = 72
NORM_EPS = 1e-05
MASKED = -1e30
LANE = 128
TILE = 384
ROWS = 32
F32 = jnp.float32
B16 = jnp.bfloat16
MESH = pl.DeviceIdType.MESH
VMEM_BYTES = 64 * 1024 * 1024


def up(n, m):
    return -(-n // m) * m


def mm(a, b):
    return lax.dot_general(a, b, (((1,), (0,)), ((), ())), preferred_element_type=F32)


def mm_nt(a, b):
    return lax.dot_general(a, b, (((1,), (1,)), ((), ())), preferred_element_type=F32)


def mm_tn(a, b):
    return lax.dot_general(a, b, (((0,), (0,)), ((), ())), preferred_element_type=F32)


def iota(shape, dim):
    return lax.broadcasted_iota(jnp.int32, shape, dim)


def onehot(mask):
    return jnp.where(mask, 1.0, 0.0).astype(B16)


def rows_of(i, n=ROWS):
    return pl.ds(pl.multiple_of(i * n, n), n)


def lanes_of(i, n=TILE):
    return pl.ds(pl.multiple_of(i * n, LANE), n)


def loop(n, body, unroll=1, first=0):
    lax.fori_loop(first, first + n, lambda i, _: (body(i), None)[1], None, unroll=unroll)


def sizes(half, width, hidden_width, dp_count):
    z = types.SimpleNamespace()
    z.half, z.D, z.FF = half, width, hidden_width
    z.HP = up(half, 16)
    z.S = 2 * z.HP
    z.SP = up(z.S, LANE)
    z.FH = hidden_width // 2
    z.DH = width // 2
    z.WS = z.DH // LANE * LANE
    z.LO = z.DH - z.WS
    z.W = width - z.WS
    z.HN = HEADS // 2
    z.HS = z.HN // 2 * HEAD_DIM
    z.SW = z.HS // LANE * LANE
    z.SL = up(z.HS + z.LO + z.HS - z.SW, LANE)
    z.PQ = up(3 * z.HS, LANE)
    z.QN = dp_count // 2
    z.QH = z.QN // 2
    z.QP = z.QN // 4
    z.bits = z.QN.bit_length() - 1
    z.far = z.bits > 3
    z.NB = 2 * z.QN
    blocks = 4 * z.QN
    z.r2, z.rs, z.rp, z.r1 = hidden_width // blocks, 2 * width // blocks, width // blocks, width // z.QN
    z.r2p, z.rsp, z.rpp, z.r1p = (up(v, 16) for v in (z.r2, z.rs, z.rp, z.r1))
    return z


def transpose_block(src, block, r, rp, shift, sp, total):
    span = min(up(r + LANE - 1, LANE), total)
    first = shift + block * r
    start = jnp.minimum(first // LANE * LANE, total - span)
    start = pl.multiple_of(start, LANE)
    row, lane = iota((rp, span), 0), iota((rp, span), 1)
    pick = onehot((lane == row + (first - start)) & (row < r))
    return mm_nt(pick, src[0:sp, pl.ds(start, span)]).astype(B16)


def jobs_of(z):
    rest = list(range(2, z.bits))
    near, far = [0, 1, *rest], [1, 0, *rest]
    jobs, base = [], 0
    for name, group, r, rp, start, n, w, parts, order in (
        ("2a", "2", z.r2, z.r2p, 0, 2 * TILE, TILE, 1, near),
        ("2b", "2", z.r2, z.r2p, 2 * TILE, z.D - 2 * TILE, TILE, 1, far),
        ("1a", "1", z.r1, z.r1p, 0, 2 * TILE, TILE, 1, near),
        ("1b", "1", z.r1, z.r1p, 2 * TILE, z.FH // 2 - 2 * TILE, TILE, 1, far),
        ("p", "p", z.rp, z.rpp, 0, z.D, TILE, 1, far),
        ("qa", "q", z.r1, z.r1p, 0, 512, 512, 1, near),
        ("qb", "q", z.r1, z.r1p, 512, z.PQ - 512, TILE, 1, far),
        ("s", "s", z.rs, z.rsp, 0, z.D, TILE, 1, near),
    ):
        jobs.append(
            types.SimpleNamespace(
                name=name, group=group, r=r, rp=rp, start=start, n=n, w=w, nt=n // w, parts=parts, order=order, base=base
            )
        )
        base += n // w * parts
    return jobs, base


GROUPS = "21pqs"


def landing_of(z):
    return {
        f"rv{j.name}{s}": ((j.nt,) + (2,) * (z.bits - 1 - s) + (j.rp, j.w), z.far)
        for j in jobs_of(z)[0]
        for s in range(z.bits)
    }


INS = (
    "lens", "tok", "sk", "cot", "sb", "g1", "h1", "pb", "g2", "h2", "b1", "b2", "sw", "qw", "pw", "f1", "f2",
)
LEFT_OUTS = ("LT2", "LT1", "LTq", "LTp", "LTs", "R1", "Rp", "Rq")


def any_outs(z):
    return LEFT_OUTS + tuple(n for n, (_, out) in landing_of(z).items() if out)


VMEM_OUTS = ("bo", "tg", "sg", "w2", "fr1", "wp", "frq", "ws", "vout")


def out_shapes(z):
    s = jax.ShapeDtypeStruct
    landing = {n: s(shape, B16) for n, (shape, _) in landing_of(z).items()}
    left = lambda rows: s((2, 2, 2, z.QP, rows, z.SP), B16)
    return landing | dict(
        LT2=left(z.r2p),
        LT1=left(z.r1p),
        LTq=left(z.r1p),
        LTp=left(z.rpp),
        LTs=left(z.rsp),
        R1=s((2, z.S, z.FH // 2), B16),
        Rp=s((2, z.S, z.D), B16),
        Rq=s((2, z.S, z.PQ), B16),
        bo=s((z.half, z.D), B16),
        tg=s((z.half, z.D), B16),
        sg=s((2 * z.half, z.DH), B16),
        w2=s((z.r2, z.D), F32),
        fr1=s((4, up(z.r1 // 4, 8), z.FH // 2), F32),
        wp=s((z.rp, z.D), F32),
        frq=s((4, up(z.r1 // 4, 8), z.PQ), F32),
        ws=s((z.rs, z.D), F32),
        vout=s((16, z.D), F32),
    )


def scratch_of(z):
    v, dma = pltpu.VMEM, pltpu.SemaphoreType.DMA
    jobs, tiles = jobs_of(z)
    out = dict(
        tokin=v((2, z.HP, z.D), B16),
        skin=v((2, z.S, z.W), B16),
        lent=v((2, 8, LANE), F32),
        dfin=v((2, z.S, z.D), B16),
        acc0=v((z.S, z.D), F32),
        acc1=v((z.S, z.D), F32),
        acc2=v((z.S, z.D), F32),
        acc3=v((z.HP, z.D), F32),
        psend=v((z.D // TILE, z.S, TILE), B16),
        pin0=v((z.D // TILE, z.S, TILE), B16),
        pin1=v((z.D // TILE, z.S, TILE), B16),
        pin3=v((z.HP, z.D), B16),
        pk=v((z.S, 3 * z.W), B16),
        probs=v((z.HN, z.S, z.S), B16),
        dact=v((z.S, z.FH), B16),
        dbase=v((2, z.S, z.D), B16),
        st2=v((4, 2, z.QP, z.r2p, z.SP), B16),
        st1=v((2, 2, z.QP, z.r1p, z.SP), B16),
        heads=v((z.SP, z.W), B16),
        bosum=v((z.HP, z.D), B16),
        rowv=v((8, z.D), F32),
        b1v=v((1, z.FF), F32),
        fbias=v((1, z.FH), F32),
        vb=v((3 + z.bits, 16, z.D), F32),
        vr=v((2 + z.bits, 16, z.D), F32),
    )
    for n, (shape, outside) in landing_of(z).items():
        if not outside:
            out[n] = v(shape, B16)
    out["wsem"] = dma((12,))
    out["lsem"] = dma((16,))
    out["ssem"], out["rsem"] = dma((64,)), dma((64,))
    out["semld"] = dma((len(GROUPS), 6))
    out["semgs"], out["semgr"] = dma((z.bits, tiles)), dma((z.bits, tiles))
    out["semfs"], out["semfr"] = dma((2, 4)), dma((2, 4))
    out["semvs"], out["semvr"] = dma((2 + z.bits,)), dma((2 + z.bits,))
    return out


def scope_one(z):
    v = pltpu.VMEM
    return dict(
        qwv=v((z.D, 3 * z.W), B16),
        pwv=v((z.W, z.D), B16),
        f1v=v((z.D, z.FH), B16),
        f2v=v((z.FH, z.D), B16),
        atile=v((z.S, TILE), F32),
        hidden=v((z.SP, z.FH), B16),
        normed=v((z.SP, z.D), B16),
        normed2=v((z.SP, z.D), B16),
        stq=v((2, 2, z.QP, z.r1p, z.SP), B16),
        sts=v((4, 2, z.QP, z.rsp, z.SP), B16),
    )


def scope_start(z):
    v = pltpu.VMEM
    return dict(
        tokpad=v((z.HP, z.D), B16),
        skpad=v((z.S, z.W), B16),
        xin=v((z.SP, z.D), B16),
    )


def scope_two(z):
    v = pltpu.VMEM
    jobs, _ = jobs_of(z)
    out = dict(
        dmidl=v((z.S, z.D), B16),
        dpack=v((z.S, 3 * z.W), B16),
        slab=v((2, z.S, z.PQ), B16),
        stp=v((4, 2, z.QP, z.rpp, z.SP), B16),
        slotl=v((1, 2, 2, 2, z.QP, max(z.r1p, z.r2p, z.rsp), z.SP), B16),
        slotr=v((1, 2 * z.SP, z.D), B16),
    )
    if z.far:
        out["zin"] = v((2 * z.QP, max(j.rp for j in jobs), 512), B16)
    for j in jobs:
        out["pr" + j.name] = v((j.nt,) + (2,) * z.bits + (j.rp, j.w), B16)
    return out


def scope_back(z):
    v = pltpu.VMEM
    return dict(qwb=v((z.D, 3 * z.W), B16), pwb=v((z.W, z.D), B16))


def scope_end(z):
    v = pltpu.VMEM
    fp = up(z.r1 // 4, 8)
    return dict(
        swb=v((z.D, z.D), B16),
        sumt=v((z.r1p, 512), F32),
        fs1=v((4, fp, z.FH // 2), F32),
        fsq=v((4, fp, z.PQ), F32),
    )


def kernel(z, *refs):
    scratch = scratch_of(z)
    r = types.SimpleNamespace(**dict(zip((*INS, *any_outs(z), *VMEM_OUTS, *scratch), refs, strict=True)))
    jobs, _ = jobs_of(z)
    j2a, j2b, j1a, j1b, jp, jqa, jqb, js = jobs
    d, x = lax.axis_index("dp"), lax.axis_index("seq")
    c, q = lax.rem(d, 2), d // 2
    bit = [lax.rem(q // 2**b, 2) for b in range(z.bits)]
    me = 2 * c + x
    peer, xpeer = (d + 1 - 2 * c, x), (d, 1 - x)
    across = [(d + (1 - 2 * bit[b]) * 2 ** (b + 1), x) for b in range(z.bits)]
    D, S, HP, half = z.D, z.S, z.HP, z.half
    nt = D // TILE

    def scoped(spec, body):
        def inner(*held):
            for name, ref in zip(spec, held, strict=True):
                setattr(r, name, ref)
            body()
            for name in spec:
                delattr(r, name)

        pl.run_scoped(inner, *spec.values())

    def quad(k):
        return (2 * q + k // 2, lax.rem(k, 2))

    def copy_to(src, dst, ss, rs, dev):
        return pltpu.make_async_remote_copy(
            src_ref=src, dst_ref=dst, send_sem=ss, recv_sem=rs, device_id=dev, device_id_type=MESH
        )

    used = [0]

    def slots(n):
        used[0] += n
        return used[0] - n

    def remote(src, dst, slot, dev):
        return copy_to(src, dst, r.ssem.at[slot], r.rsem.at[slot], dev)

    def wait_recv(dst, slot):
        remote(dst, dst, slot, xpeer).wait_recv()

    def wait_send(src, slot):
        remote(src, src, slot, xpeer).wait_send()

    def local(src, dst, n):
        return pltpu.make_async_copy(src, dst, r.lsem.at[n])

    def load(src, dst, n):
        return pltpu.make_async_copy(src, dst, r.wsem.at[n])

    def at16(start, n):
        return pl.ds(pl.multiple_of(start, 16), n)

    def at128(start, n):
        return pl.ds(pl.multiple_of(start, LANE), n)

    hx, hx1, hc, hc1 = (at16(HP * v, HP) for v in (x, 1 - x, c, 1 - c))

    S_LEN, S_TOK, S_SK, S_COT, S_P0, S_P1, S_P2, S_P4 = (slots(n) for n in (1, 2, 2, 3, nt, nt, nt, nt))
    S_P3, S_TS, S_TP, S_T2, S_XQ, S_X1, S_XP, S_XS, S_R1, S_RQ, S_BO = (
        slots(n) for n in (1, 3, 3, 6, 2, 2, 2, 2, 1, 1, 1)
    )

    barrier = pltpu.get_barrier_semaphore()
    for t in range(1, 4):
        pl.semaphore_signal(barrier, inc=1, device_id=quad(lax.rem(me + t, 4)), device_id_type=MESH)
    for other in across:
        pl.semaphore_signal(barrier, inc=1, device_id=other, device_id_type=MESH)
    pl.semaphore_wait(barrier, 3 + z.bits)

    def qkv_loads(dst):
        return [
            load(r.qw.at[:, at128(D * j + z.WS * c, z.W)], dst.at[:, z.W * j : z.W * (j + 1)], 1 + j) for j in range(3)
        ]

    def proj_load(dst):
        return load(r.pw.at[at16(z.WS * c, z.W), :], dst, 4)

    def partial_sums(value, mine, theirs, slot):
        def step(i):
            v = value(i)
            at = lanes_of(i)
            mine[:, at] = v
            r.psend[i] = v.astype(B16)
            remote(r.psend.at[i], theirs.at[i], slot + i, peer).start()

        loop(nt, step)

    def partial_done(theirs, slot):
        def step(i):
            remote(r.psend.at[i], theirs.at[i], slot + i, peer).wait()

        loop(nt, step)

    def spread_blocks(src, stage, rr, rrp, shift, out, slot, lslot, part=0, parts=1):
        n = z.NB // parts
        known = src.shape[1] * (part + 1) // parts

        def step(b):
            m = b // 4
            stage[lax.rem(b, 4), m // z.QP, lax.rem(m, z.QP)] = transpose_block(src, b, rr, rrp, shift, z.SP, known)

        loop(n, step, 4, part * n)
        some = slice(part, part + 1) if parts > 1 else slice(0, 2)
        for t in range(1, 4):
            k = lax.rem(me + t, 4)
            remote(stage.at[k, some], out.at[x, c, some], slot + part * 3 + t - 1, quad(k)).start()
        local(stage.at[me, some], out.at[x, c, some], lslot + part).start(priority=1)

    def spread_sent(stage, out, slot, lslot, parts=1):
        n = 2 // parts
        for i in range(3 * parts):
            wait_send(stage.at[0, 0:n], slot + i)
        for part in range(parts):
            local(stage.at[0, 0:n], out.at[x, 0, 0:n], lslot + part).wait()

    def spread_here(out, slot, part=0, parts=1):
        for i in range(3):
            wait_recv(out.at[x, 0, 0 : 2 // parts], slot + part * 3 + i)

    def whole_blocks(src, stage, out, slot, lslot):
        def step(b):
            stage[b // (2 * z.QP), lax.rem(b // z.QP, 2), lax.rem(b, z.QP)] = transpose_block(
                src, b, z.r1, z.r1p, 0, z.SP, D
            )

        loop(z.QN, step, 4)
        remote(stage.at[c], out.at[x, c], slot, xpeer).start()
        local(stage, out.at[x], lslot).start(priority=1)

    def relay(out, part, slot):
        wait_recv(out.at[1 - x, part], slot)
        remote(out.at[1 - x, part], out.at[1 - x, part], slot + 1, peer).start()

    def whole(tiles, at):
        return jnp.concatenate([tiles[t, at] for t in range(nt)], axis=1).astype(F32)

    def normalise(v, gain, shift):
        mean = jnp.mean(v, axis=-1, keepdims=True)
        centred = v - mean
        var = jnp.mean(centred * centred, axis=-1, keepdims=True)
        return centred * lax.rsqrt(var + NORM_EPS) * gain + shift

    def norm_back(v, dn, gain):
        mean = jnp.mean(v, axis=-1, keepdims=True)
        centred = v - mean
        var = jnp.mean(centred * centred, axis=-1, keepdims=True)
        rstd = lax.rsqrt(var + NORM_EPS)
        hat = centred * rstd
        dh = dn * gain
        one = jnp.mean(dh, axis=-1, keepdims=True)
        two = jnp.mean(dh * hat, axis=-1, keepdims=True)
        return rstd * (dh - one - hat * two), dn * hat

    def fold(v):
        return jnp.sum(v, axis=0, keepdims=True)

    zero = jnp.zeros((1, D), F32)
    SB, G1, H1, PB, G2, H2, B2 = range(7)

    def rowp(i):
        return r.rowv[i : i + 1, :]

    tok_self, sk_self = (c == 0) & (x == 0), (c == 1) & (x == 1)
    span = 2 * LANE
    scale = HEAD_DIM ** (-0.5)

    def head_window(h):
        first = z.LO * c + HEAD_DIM * h
        start = pl.multiple_of(jnp.minimum(first // LANE * LANE, z.W - span), LANE)
        lane = iota((1, span), 1) + start
        keep = jnp.where((lane >= first) & (lane < first + HEAD_DIM), 1.0, 0.0)
        return start, keep

    def length_here():
        return jnp.where(c == x, r.lent[0], r.lent[1])[0:1, 0:1]

    def begin():
        load(r.sw.at[at16(D * c, D)], r.f1v.at[:, 0:D], 0).start(priority=1)
        for v in qkv_loads(r.qwv):
            v.start(priority=1)
        proj_load(r.pwv).start(priority=1)
        length = r.lens[0].astype(F32)
        r.lent[0] = jnp.full((8, LANE), length, F32)
        remote(r.lent.at[0], r.lent.at[1], S_LEN, peer).start()
        spread = onehot((iota((HP, half), 0) == iota((HP, half), 1)))
        r.tokpad[...] = mm(spread, r.tok[...]).astype(B16)

        @pl.when(tok_self)
        def _():
            r.tokin[x] = r.tokpad[...]

        @pl.when(jnp.logical_not(tok_self))
        def _():
            remote(r.tokpad, r.tokin.at[x], S_TOK + x, quad(c)).start()

        row, col = iota((S, 2 * half), 0), iota((S, 2 * half), 1)
        pick = onehot(((row < half) & (row == col)) | ((row >= HP) & (row < HP + half) & (col == row - (HP - half))))
        shift = onehot(iota((z.DH, z.W), 1) == iota((z.DH, z.W), 0) + z.LO * x)
        r.skpad[...] = mm(mm(pick, r.sk[...]).astype(B16), shift).astype(B16)

        @pl.when(sk_self)
        def _():
            r.skin[x] = r.skpad[...]

        @pl.when(jnp.logical_not(sk_self))
        def _():
            remote(r.skpad, r.skin.at[x], S_SK + x, quad(2 + c)).start()

        own_row = iota((HP, 1), 0)
        live = (own_row < half) & ((own_row + half * x).astype(F32) < length)
        r.dfin[c, hx] = jnp.where(live, mm(spread, r.cot[...]), 0.0).astype(B16)

        for ref in (r.xin, r.normed, r.normed2, r.hidden):
            ref[S:, :] = jnp.zeros((z.SP - S, ref.shape[1]), B16)
        r.heads[...] = jnp.zeros(r.heads.shape, B16)
        for i, ref in enumerate((r.sb, r.g1, r.h1, r.pb, r.g2, r.h2, r.b2)):
            r.rowv[i : i + 1, :] = ref[...].astype(F32).reshape(1, D)
        r.b1v[...] = r.b1[...].astype(F32).reshape(1, z.FF)

        for h in range(2):
            @pl.when((c == 0) & jnp.logical_not(tok_self & (h == 0)))
            def _(h=h):
                wait_recv(r.tokin.at[h], S_TOK + h)

            @pl.when((c == 1) & jnp.logical_not(sk_self & (h == 1)))
            def _(h=h):
                wait_recv(r.skin.at[h], S_SK + h)

        remote(r.dfin.at[c, hx], r.dfin.at[c, hx], S_COT, xpeer).start()
        remote(r.dfin.at[c, hx], r.dfin.at[c, hx], S_COT + 1, peer).start()

        @pl.when(c == 0)
        def _():
            for h in range(2):
                r.xin[h * HP : (h + 1) * HP, :] = r.tokin[h]

        @pl.when(c == 1)
        def _():
            r.xin[0:S, 0 : z.WS] = r.skin[0, :, 0 : z.WS]
            r.xin[0:S, z.WS : z.W] = r.skin[0, :, z.WS : z.W] + r.skin[1, :, 0 : z.W - z.WS]
            r.xin[0:S, z.W : D] = r.skin[1, :, z.W - z.WS : z.W]

        load(r.sw.at[at16(D * c, D)], r.f1v.at[:, 0:D], 0).wait()
        partial_sums(lambda i: mm(r.xin[0:S], r.f1v[:, lanes_of(i)]), r.acc0, r.pin0, S_P0)
        spread_blocks(r.xin, r.sts, z.rs, z.rsp, 0, r.LTs, S_TS, 0)

        @pl.when(jnp.logical_not(tok_self))
        def _():
            wait_send(r.tokpad, S_TOK + x)

        @pl.when(jnp.logical_not(sk_self))
        def _():
            wait_send(r.skpad, S_SK + x)

    def ff_loads():
        return [load(r.f1.at[:, at128(z.FH * c, z.FH)], r.f1v, 5), load(r.f2.at[at16(z.FH * c, z.FH), :], r.f2v, 6)]

    def forward():
        scoped(scope_start(z), begin)
        for v in ff_loads():
            v.start(priority=1)
        partial_done(r.pin0, S_P0)

        def norm_one(i):
            at = rows_of(i)
            v = r.acc0[at] + whole(r.pin0, at) + rowp(SB)
            r.acc0[at] = v
            r.normed[at] = normalise(v, rowp(G1), rowp(H1)).astype(B16)

        loop(S // ROWS, norm_one, S // ROWS)
        for v in qkv_loads(r.qwv):
            v.wait()

        def qkv_tile(i):
            r.pk[:, lanes_of(i)] = mm(r.normed[0:S], r.qwv[:, lanes_of(i)]).astype(B16)

        loop(3 * z.W // TILE, qkv_tile)

        wait_recv(r.dfin.at[c, hx1], S_COT)
        remote(r.dfin.at[c, hx1], r.dfin.at[c, hx1], S_COT + 2, peer).start()

        wait_recv(r.lent.at[1], S_LEN)
        slot_col = iota((1, S), 1)
        slot_of = jnp.where(slot_col < HP, slot_col, slot_col - (HP - half))
        key_ok = ((slot_col < half) | ((slot_col >= HP) & (slot_col < HP + half))) & (
            slot_of.astype(F32) < length_here()
        )

        def head_forward(h):
            start, keep = head_window(h)
            query = r.pk[:, pl.ds(start, span)] * keep.astype(B16)
            key = r.pk[:, at128(z.W + start, span)]
            value = r.pk[:, at128(2 * z.W + start, span)]
            scores = jnp.where(key_ok, mm_nt(query, key) * scale, MASKED)
            top = jnp.max(scores, axis=-1, keepdims=True)
            e = jnp.exp(scores - top)
            probs = (e * (1.0 / jnp.sum(e, axis=-1, keepdims=True))).astype(B16)
            r.probs[h] = probs
            at = pl.ds(start, span)
            r.heads[0:S, at] = r.heads[0:S, at] + (mm(probs, value) * keep).astype(B16)

        loop(z.HN, head_forward, 2)

        proj_load(r.pwv).wait()
        partial_sums(lambda i: mm(r.heads[0:S], r.pwv[:, lanes_of(i)]), r.acc1, r.pin1, S_P1)
        whole_blocks(r.normed, r.stq, r.LTq, S_XQ, 1)
        partial_done(r.pin1, S_P1)

        def norm_two(i):
            at = rows_of(i)
            v = r.acc0[at] + r.acc1[at] + whole(r.pin1, at) + rowp(PB)
            r.acc1[at] = v
            r.normed2[at] = normalise(v, rowp(G2), rowp(H2)).astype(B16)

        loop(S // ROWS, norm_two, S // ROWS)

        whole_blocks(r.normed2, r.st1, r.LT1, S_X1, 4)
        wait_recv(r.dfin.at[1 - c, hx], S_COT + 1)
        wait_recv(r.dfin.at[1 - c, hx1], S_COT + 2)
        for v in ff_loads():
            v.wait()

        def hidden_tile(i):
            at = lanes_of(i)
            a = mm(r.normed2[0:S], r.f1v[:, at]) + r.b1v[:, at128(z.FH * c + i * TILE, TILE)]
            dh = mm_nt(r.dfin[x], r.f2v[rows_of(i, TILE), :])
            cdf = 0.5 * (1.0 + lax.erf(a * (2.0**-0.5)))
            pdf = jnp.exp(-0.5 * a * a) * (0.5 / jnp.pi) ** 0.5
            r.hidden[0:S, at] = (a * cdf).astype(B16)
            da = dh * (cdf + a * pdf)
            r.dact[:, at] = da.astype(B16)
            r.fbias[:, at] = fold(da)

        tiles, fq = z.FH // TILE // 2, z.FH // 2
        loop(tiles, lambda i: hidden_tile(tiles * (1 - x) + i), tiles)
        remote(r.dact.at[:, at128(fq * (1 - x), fq)], r.R1.at[x], S_R1, xpeer).start()
        relay(r.LTq, c, S_XQ)
        relay(r.LT1, c, S_X1)
        loop(tiles, lambda i: hidden_tile(tiles * x + i), tiles)
        partial_sums(lambda i: mm_nt(r.dact[...], r.f1v[rows_of(i, TILE), :]), r.acc2, r.pin0, S_P2)
        spread_blocks(r.hidden, r.st2, z.r2, z.r2p, 0, r.LT2, S_T2, 8)
        local(r.dact.at[:, at128(fq * x, fq)], r.R1.at[x], 3).start(priority=1)

        def result_tile(i):
            at = lanes_of(i)
            r.atile[...] = mm(r.hidden[0:S], r.f2v[:, at])
            r.acc3[:, at] = r.atile[hc]
            r.tokin[0, :, at] = r.atile[hc1].astype(B16)

        loop(nt, result_tile)
        remote(r.tokin.at[0], r.pin3, S_P3, peer).start()
        spread_sent(r.sts, r.LTs, S_TS, 0)
        wait_send(r.stq.at[c], S_XQ)
        local(r.stq, r.LTq.at[x], 1).wait()

    def ref(kind, j):
        return getattr(r, kind + j.name)

    def tile(j, i):
        return at128(j.start + i * j.w, j.w)

    def group_loads(j, part):
        n = GROUPS.index(j.group)
        s = n % r.slotl.shape[0]
        left = getattr(r, "LT" + j.group)
        right = {"2": r.dfin, "1": r.R1, "p": r.Rp, "q": r.Rq, "s": r.dbase}[j.group]
        some = slice(0, 2) if part is None else slice(part, part + 1)
        for i in range(2):
            yield pltpu.make_async_copy(
                left.at[i, :, some], r.slotl.at[s, i, :, some, :, 0 : j.rp], r.semld.at[n, 2 * (part or 0) + i]
            )
            if not part:
                yield pltpu.make_async_copy(
                    right.at[i], r.slotr.at[s, i * z.SP : i * z.SP + S, 0 : right.shape[-1]], r.semld.at[n, 4 + i]
                )

    def kept(j, s, keep, part=None):
        at = [slice(None)] * z.bits
        for b in j.order[:s]:
            at[z.bits - 1 - b] = bit[b]
        b = j.order[s]
        at[z.bits - 1 - b] = bit[b] if keep else 1 - bit[b]
        if part is not None:
            at[1] = slice(part, part + 1)
        return tuple(at)

    def landed(j, s):
        return getattr(r, f"rv{j.name}{s}")

    def half_copy(j, s, i, part=0):
        split = s == 0 and j.parts > 1
        src = ref("pr", j).at[(i, *kept(j, s, False, part if split else None))]
        dst = landed(j, s)
        lead = (i, slice(None), slice(part, part + 1)) if split else (i,)
        n = j.base + part * j.nt + i
        return copy_to(src, dst.at[lead], r.semgs.at[s, n], r.semgr.at[s, n], across[j.order[s]])

    def prep(j, part=None):
        for v in group_loads(j, part):
            v.start(priority=1)

    def ready(j, part=None):
        for v in group_loads(j, part):
            v.wait()

    def products(j, part=0):
        s = GROUPS.index(j.group) % r.slotl.shape[0]

        def step(i):
            at = tile(j, i)
            if j.parts > 1:
                left = [r.slotl[s, n, :, part, :, 0 : j.rp] for n in range(2)]
                to = (slice(None), part)
            else:
                left = [r.slotl[s, n, :, :, :, 0 : j.rp] for n in range(2)]
                to = ()
            left = [v.reshape(z.QN // j.parts * j.rp, z.SP) for v in left]
            out = mm(jnp.concatenate(left, axis=1), r.slotr[s, :, at])
            shape = (2,) * (z.bits - (j.parts > 1)) + (j.rp, j.w)
            ref("pr", j)[(i, *to)] = out.astype(B16).reshape(shape)
            half_copy(j, 0, i, part).start()

        loop(j.nt, step)

    def sums(j, s, store=None):
        def step(i):
            at = tile(j, i)
            for part in range(j.parts if s == 0 else 1):
                half_copy(j, s, i, part).wait_recv()
            here = (i, *kept(j, s, True))
            theirs = landed(j, s)
            if z.far:
                n = 2 ** (z.bits - 1 - s)
                stage = r.zin.at[0:n, 0 : j.rp, 0 : j.w]
                for k in range(n):
                    pick = tuple(k // 2**b % 2 for b in reversed(range(z.bits - 1 - s)))
                    fetch = local(theirs.at[(i, *pick)], stage.at[k], 15)
                    fetch.start()
                    fetch.wait()
                piece = stage[...].reshape(theirs.shape[1:])
            else:
                piece = theirs[i]
            total = ref("pr", j)[here].astype(F32) + piece.astype(F32)
            if s < z.bits - 1:
                ref("pr", j)[here] = total.astype(B16)
                half_copy(j, s + 1, i).start()
            else:
                store(at, total)

        loop(j.nt, step)

    def more_sums(j):
        for s in range(2, z.bits - 1):
            sums(j, s)

    def sums_sent(j):
        def step(i):
            for s in range(z.bits):
                for part in range(j.parts if s == 0 else 1):
                    half_copy(j, s, i, part).wait_send()

        loop(j.nt, step)

    rq = z.r1 // 4

    def fix_copy(n, g, t):
        k = lax.rem(me + t, 4)
        src, dst = getattr(r, "fs" + g), getattr(r, "fr" + g)
        return copy_to(src.at[k], dst.at[me], r.semfs.at[n, t - 1], r.semfr.at[n, t - 1], quad(k))

    def fix_start(n, g):
        for t in range(1, 4):
            fix_copy(n, g, t).start()
        getattr(r, "fr" + g)[me] = getattr(r, "fs" + g)[me]

    def fix_wait(n, g):
        for t in range(1, 4):
            fix_copy(n, g, t).wait()

    def direct(out):
        def store(at, total):
            out[:, at] = total[0 : out.shape[0]]

        return store

    def summed(out):
        def store(at, total):
            w = total.shape[1]
            r.sumt[:, 0:w] = total
            for k in range(4):
                out[k, 0:rq, at] = r.sumt[k * rq : (k + 1) * rq, 0:w]

        return store

    v_devs = (peer, xpeer, *across)

    def v_copy(s):
        return copy_to(r.vb.at[s], r.vr.at[s], r.semvs.at[s], r.semvr.at[s], v_devs[s])

    def v_step(s):
        if s > 0:
            v_copy(s - 1).wait()
            r.vb[s] = r.vb[s - 1] + r.vr[s - 1]
        if s < len(v_devs):
            v_copy(s).start()

    def back():
        for v in qkv_loads(r.qwb):
            v.start(priority=1)
        proj_load(r.pwb).start(priority=1)
        for s in range(r.slotr.shape[0]):
            for i in range(2):
                r.slotr[s, i * z.SP + S : (i + 1) * z.SP, :] = jnp.zeros((z.SP - S, D), B16)
        r.dpack[...] = jnp.zeros(r.dpack.shape, B16)
        partial_done(r.pin0, S_P2)

        def norm_two_back(i, sums):
            at = rows_of(i)
            dn = r.acc2[at] + whole(r.pin0, at)
            dv, dg = norm_back(r.acc1[at], dn, rowp(G2))
            df = r.dfin[x, at].astype(F32)
            dm = df + dv
            r.acc2[at] = dm
            r.dmidl[at] = dm.astype(B16)
            return sums[0] + fold(dg), sums[1] + fold(dn), sums[2] + fold(df), sums[3] + fold(dm)

        dg2, dh2, db2, dpb = lax.fori_loop(0, S // ROWS, norm_two_back, (zero, zero, zero, zero), unroll=S // ROWS)
        local(r.dmidl, r.Rp.at[x], 6).start(priority=1)
        wait_recv(r.LT1.at[1 - x, 1 - c], S_X1 + 1)
        local(r.st1, r.LT1.at[x], 4).wait()
        wait_recv(r.R1.at[1 - x], S_R1)
        local(r.R1.at[x], r.R1.at[x], 3).wait()
        prep(j1a)
        r.vb[0] = jnp.zeros((16, D), F32)
        first = jnp.where(c == 0, 1.0, 0.0)
        for i, v in ((3, dpb), (4, dg2), (5, dh2), (6, db2)):
            r.vb[0, i : i + 1, :] = v * first
        for j in range(z.FH // D):
            v = r.fbias[:, j * D : (j + 1) * D]
            r.vb[0, 8 + j : 9 + j, :] = v * first
            r.vb[0, 10 + j : 11 + j, :] = v * (1.0 - first)

        proj_load(r.pwb).wait()
        r.skin[0] = mm_nt(r.dmidl[...], r.pwb[...]).astype(B16)
        ready(j1a)
        products(j1a)
        products(j1b)

        def head_backward(h):
            start, keep = head_window(h)
            low = keep.astype(B16)
            at_q, at_k, at_v = pl.ds(start, span), at128(z.W + start, span), at128(2 * z.W + start, span)
            query, key, value = r.pk[:, at_q], r.pk[:, at_k], r.pk[:, at_v]
            dh = r.skin[0, :, at_q]
            probs = r.probs[h]
            dp = mm_nt(dh * low, value)
            pf = probs.astype(F32)
            delta = jnp.sum(dp * pf, axis=-1, keepdims=True)
            ds = (pf * (dp - delta) * scale).astype(B16)
            r.dpack[:, at_q] = r.dpack[:, at_q] + (mm(ds, key) * keep).astype(B16)
            r.dpack[:, at_k] = r.dpack[:, at_k] + (mm_tn(ds, query) * keep).astype(B16)
            r.dpack[:, at_v] = r.dpack[:, at_v] + (mm_tn(probs, dh) * keep).astype(B16)

        def slab_of(mine, part):
            first = z.LO * c + (z.HS - z.SW) * part
            row, lane = iota((z.SL, z.SL), 0), iota((z.SL, z.SL), 1)
            out = []
            for t in range(3):
                to = z.HS * t // LANE * LANE
                move = onehot((row - first == lane - (z.HS * t - to)) & (row >= first) & (row < first + z.HS))
                out.append((to, mm(r.dpack[:, at128(z.W * t + z.SW * part, z.SL)], move).astype(B16)))
            for at in range(0, z.PQ, LANE):
                held = [v[:, at - to : at - to + LANE] for to, v in out if to <= at < to + z.SL]
                r.slab[mine, :, at : at + LANE] = held[0] if len(held) == 1 else held[0] + held[1]

        nh = z.HN // 2
        loop(nh, lambda i: head_backward(nh * (1 - x) + i), 2)
        slab_of(0, 1 - x)
        remote(r.slab.at[0], r.Rq.at[x], S_RQ, xpeer).start()
        remote(r.dmidl.at[hc], r.Rp.at[x, hc], S_XP, xpeer).start()
        block_out()
        spread_here(r.LT2, S_T2)
        local(r.st2.at[0], r.LT2.at[x, 0], 8).wait()
        prep(j2a)
        ready(j2a)
        products(j2a)
        products(j2b)
        loop(nh, lambda i: head_backward(nh * x + i), 2)
        for v in qkv_loads(r.qwb):
            v.wait()
        partial_sums(lambda i: mm_nt(r.dpack[...], r.qwb[rows_of(i, TILE), :]), r.acc1, r.pin1, S_P4)
        slab_of(1, x)
        local(r.slab.at[1], r.Rq.at[x], 7).start(priority=1)
        spread_blocks(r.heads, r.stp, z.rp, z.rpp, z.LO * c, r.LTp, S_TP, 2)
        sums(j1a, 0)
        sums(j1b, 0)
        relay(r.Rp, hc, S_XP)

    def block_out():
        wait_recv(r.pin3, S_P3)
        slot_row = iota((HP, 1), 0)
        out_ok = (slot_row < half) & ((slot_row + half * c).astype(F32) < length_here())
        total = r.acc1[hc] + r.acc3[...] + r.pin3[...].astype(F32) + rowp(B2)
        r.tokin[1] = jnp.where(out_ok, total, 0.0).astype(B16)

        @pl.when(c == x)
        def _():
            r.bosum[...] = r.tokin[1]

    def finish():
        weight = [
            load(r.sw.at[0:D], r.swb, 8),
            load(r.sw.at[at16(D + z.DH * x, z.DH)], r.swb.at[0 : z.DH], 9),
        ]
        weight[0].start(priority=1)
        partial_done(r.pin1, S_P4)

        def norm_one_back(i, sums):
            at = rows_of(i)
            dn = r.acc1[at] + whole(r.pin1, at)
            dv, dg = norm_back(r.acc0[at], dn, rowp(G1))
            db = r.acc2[at] + dv
            r.dbase[x, at] = db.astype(B16)
            return sums[0] + fold(dg), sums[1] + fold(dn), sums[2] + fold(db)

        dg1, dh1, dsb = lax.fori_loop(0, S // ROWS, norm_one_back, (zero, zero, zero), unroll=S // ROWS)
        first = jnp.where(c == 0, 1.0, 0.0)
        for i, v in enumerate((dsb, dg1, dh1)):
            r.vb[0, i : i + 1, :] = v * first
        v_step(0)

        remote(r.dbase.at[x, hc], r.dbase.at[x, hc], S_XS, xpeer).start()
        wait_recv(r.LTq.at[1 - x, 1 - c], S_XQ + 1)
        wait_recv(r.Rq.at[1 - x], S_RQ)
        local(r.Rq.at[x], r.Rq.at[x], 7).wait()
        prep(jqa)
        ready(jqa)
        products(jqa)
        products(jqb)
        wait_recv(r.Rp.at[1 - x, hc1], S_XP + 1)
        local(r.dmidl, r.Rp.at[x], 6).wait()
        spread_here(r.LTp, S_TP)
        spread_sent(r.stp, r.LTp, S_TP, 2)
        prep(jp)
        v_step(1)
        sums(j2b, 0)
        sums(j1b, 1)
        ready(jp)
        products(jp)
        sums(j1a, 1)
        relay(r.dbase, hc, S_XS)
        spread_here(r.LTs, S_TS)
        sums(j2a, 0)
        wait_recv(r.dbase.at[1 - x, hc1], S_XS + 1)
        prep(js)
        v_step(2)

        @pl.when(c != x)
        def _():
            remote(r.tokin.at[1], r.bosum, S_BO, (2 * q + x, c)).start()

        ready(js)
        products(js)
        more_sums(j1a)
        more_sums(j1b)
        v_step(3)
        sums(j2b, 1)
        sums(jp, 0)
        sums(jqb, 0)
        sums(j1b, z.bits - 1, summed(r.fs1))
        weight[0].wait()
        r.tg[...] = mm_nt(r.dbase[c, hx], r.swb[...]).astype(B16)[0:half]
        weight[1].start(priority=1)
        v_step(4)
        sums(j1a, z.bits - 1, summed(r.fs1))
        fix_start(0, "1")
        sums(j2a, 1)
        sums(jqa, 0)
        more_sums(j2a)
        more_sums(j2b)
        sums(j2b, z.bits - 1, direct(r.w2))
        weight[1].wait()
        sg = mm_nt(r.dbase[c], r.swb[0 : z.DH, :]).astype(B16)
        row, col = iota((2 * half, S), 0), iota((2 * half, S), 1)
        back_rows = onehot(((row < half) & (row == col)) | ((row >= half) & (col == row + (HP - half))))
        r.sg[...] = mm(back_rows, sg).astype(B16)
        for s in range(5, len(v_devs) + 1):
            v_step(s)
        r.vout[...] = r.vb[len(v_devs)]
        sums(jqb, 1)
        more_sums(jqb)
        sums(jp, 1)
        more_sums(jp)
        sums(js, 0)
        sums(j2a, z.bits - 1, direct(r.w2))

        @pl.when(c == x)
        def _():
            r.bosum[...] = r.tokin[1]

        @pl.when(c != x)
        def _():
            remote(r.tokin.at[1], r.bosum, S_BO, (2 * q + x, c)).wait()

        r.bo[...] = r.bosum[0:half]
        sums(jqa, 1)
        more_sums(jqa)
        sums(jqb, z.bits - 1, summed(r.fsq))
        fix_wait(0, "1")
        sums(jp, z.bits - 1, direct(r.wp))
        sums(js, 1)
        more_sums(js)
        sums(jqa, z.bits - 1, summed(r.fsq))
        fix_start(1, "q")
        sums(js, z.bits - 1, direct(r.ws))
        fix_wait(1, "q")

        wait_send(r.lent.at[0], S_LEN)
        for j in range(3):
            wait_send(r.dfin.at[c, hx], S_COT + j)
        for j in range(3):
            wait_send(r.st2.at[0], S_T2 + j)
        wait_send(r.tokin.at[0], S_P3)
        wait_send(r.st1.at[c], S_X1)
        wait_send(r.dmidl.at[hc], S_XP)
        wait_send(r.dbase.at[x, hc], S_XS)
        wait_send(r.LTq.at[1 - x, c], S_XQ + 1)
        wait_send(r.LT1.at[1 - x, c], S_X1 + 1)
        wait_send(r.Rp.at[1 - x, hc], S_XP + 1)
        wait_send(r.dbase.at[1 - x, hc], S_XS + 1)
        wait_send(r.R1.at[x], S_R1)
        wait_send(r.slab.at[0], S_RQ)
        for j in jobs:
            sums_sent(j)

    def backward():
        scoped(scope_back(z), back)
        scoped(scope_end(z), finish)

    scoped(scope_one(z), forward)
    scoped(scope_two(z), backward)


def call(z, *args):
    outs = out_shapes(z)
    anywhere, vmem = pl.BlockSpec(memory_space=pl.ANY), pl.BlockSpec(memory_space=pltpu.VMEM)
    names = (*any_outs(z), *VMEM_OUTS)
    res = pl.pallas_call(
        functools.partial(kernel, z),
        out_shape=[outs[n] for n in names],
        in_specs=[pl.BlockSpec(memory_space=pltpu.SMEM), *([vmem] * 11), *([anywhere] * 5)],
        out_specs=[anywhere] * len(any_outs(z)) + [vmem] * len(VMEM_OUTS),
        scratch_shapes=list(scratch_of(z).values()),
        compiler_params=pltpu.CompilerParams(
            collective_id=0, has_side_effects=True, vmem_limit_bytes=VMEM_BYTES
        ),
        name="block",
    )(*args)
    return dict(zip(names, res))


def place(z, bo, tg, sg, w2, fr1, wp, frq, ws, vout, *outs):
    (bo_o, tg_o, sg_o, ws_o, sb_o, g1_o, h1_o, wq_o, wp_o, pb_o, g2_o, h2_o, w1_o, b1_o, w2_o, b2_o) = outs
    for src, dst in ((bo, bo_o), (tg, tg_o), (sg, sg_o), (ws, ws_o), (wp, wp_o), (w2, w2_o)):
        dst[...] = src[...]
    rq, fq = z.r1 // 4, z.FH // 2
    for k in range(4):
        w1_o[:, k * fq : (k + 1) * fq] = fr1[k, 0:rq]
    for t in range(3):
        wq_o[:, t * z.D : (t + 1) * z.D] = jnp.concatenate(
            [frq[k, 0:rq, t * z.HS : (t + 1) * z.HS] for k in range(4)], axis=1
        )
    block = 2 * lax.axis_index("dp") + lax.axis_index("seq")

    def take(v, first, n):
        pick = jnp.where(iota((z.D, n), 0) == iota((z.D, n), 1) + first, 1.0, 0.0)
        return lax.dot_general(
            v, pick, (((1,), (0,)), ((), ())), preferred_element_type=F32, precision=lax.Precision.HIGHEST
        )

    own = take(vout[0:8], block * z.rp, z.rp)
    for i, dst in enumerate((sb_o, g1_o, h1_o, pb_o, g2_o, h2_o, b2_o)):
        dst[...] = own[i : i + 1, :].reshape(z.rp)
    per = z.D // z.r2
    row = iota((8, z.D), 0)
    held = jnp.where(row == block // per, vout[8:16], 0.0)
    b1_o[...] = jnp.sum(take(held, lax.rem(block, per) * z.r2, z.r2), axis=0, keepdims=True).reshape(z.r2)


def call_place(z, g):
    s = jax.ShapeDtypeStruct
    one = s((z.rp,), F32)
    vmem = pl.BlockSpec(memory_space=pltpu.VMEM)
    res = [
        s((z.half, z.D), B16), s((z.half, z.D), B16), s((2 * z.half, z.DH), B16), s((z.rs, z.D), F32), one, one, one,
        s((z.r1 // 4, 3 * z.D), F32), s((z.rp, z.D), F32), one, one, one, s((z.r1 // 4, z.FF), F32), s((z.r2,), F32),
        s((z.r2, z.D), F32), one,
    ]
    return pl.pallas_call(
        functools.partial(place, z),
        out_shape=res,
        in_specs=[vmem] * len(VMEM_OUTS),
        out_specs=[vmem] * len(res),
        compiler_params=pltpu.CompilerParams(vmem_limit_bytes=32 * 1024 * 1024),
        name="place",
    )(*(g[n] for n in VMEM_OUTS))


def shards(tokens, skip_feats, lengths, cotangent, skip_weight, skip_bias, norm1_gain, norm1_bias, qkv_weight,
           proj_weight, proj_bias, norm2_gain, norm2_bias, fc1_weight, fc1_bias, fc2_weight, fc2_bias):
    dp_count = lax.axis_size("dp")
    half, width = tokens.shape[1:]
    z = sizes(half, width, fc1_weight.shape[1], dp_count)
    g = call(z, lengths, tokens[0], skip_feats[0], cotangent[0], skip_bias, norm1_gain, norm1_bias, proj_bias,
             norm2_gain, norm2_bias, fc1_bias, fc2_bias, skip_weight, qkv_weight, proj_weight, fc1_weight, fc2_weight)
    out = call_place(z, g)
    return (*(v[None] for v in out[:3]), *out[3:])


def solution(mesh):
    placed = (P("dp", "seq", None), P("dp", None, "seq"), P("dp"), P("dp", "seq", None), *([P()] * 13))
    both = ("dp", "seq")
    return jax.shard_map(
        shards, mesh=mesh, in_specs=placed,
        out_specs=(P("dp", "seq", None), P("dp", "seq", None), P("dp", None, "seq"), P(both, None), P(both), P(both),
                   P(both), P(both, None), P(both, None), P(both), P(both), P(both), P(both, None), P(both),
                   P(both, None), P(both)),
        check_vma=False,
    )
```

```python
import functools
import types

import jax
import jax.numpy as jnp
from jax import lax
from jax.experimental import pallas as pl
from jax.experimental.pallas import tpu as pltpu
from jax.sharding import PartitionSpec as P

HEADS = 16
HEAD_DIM = 72
NORM_EPS = 1e-05
MASKED = -1e30
LANE = 128
TILE = 384
ROWS = 32
F32 = jnp.float32
B16 = jnp.bfloat16
MESH = pl.DeviceIdType.MESH
VMEM_BYTES = 64 * 1024 * 1024


def up(n, m):
    return -(-n // m) * m


def mm(a, b):
    return lax.dot_general(a, b, (((1,), (0,)), ((), ())), preferred_element_type=F32)


def mm_nt(a, b):
    return lax.dot_general(a, b, (((1,), (1,)), ((), ())), preferred_element_type=F32)


def mm_tn(a, b):
    return lax.dot_general(a, b, (((0,), (0,)), ((), ())), preferred_element_type=F32)


def iota(shape, dim):
    return lax.broadcasted_iota(jnp.int32, shape, dim)


def onehot(mask):
    return jnp.where(mask, 1.0, 0.0).astype(B16)


def rows_of(i, n=ROWS):
    return pl.ds(pl.multiple_of(i * n, n), n)


def lanes_of(i, n=TILE):
    return pl.ds(pl.multiple_of(i * n, LANE), n)


def loop(n, body, unroll=1, first=0):
    lax.fori_loop(first, first + n, lambda i, _: (body(i), None)[1], None, unroll=unroll)


def sizes(half, width, hidden_width, dp_count):
    z = types.SimpleNamespace()
    z.half, z.D, z.FF = half, width, hidden_width
    z.HP = up(half, 16)
    z.S = 2 * z.HP
    z.SP = up(z.S, LANE)
    z.FH = hidden_width // 2
    z.DH = width // 2
    z.WS = z.DH // LANE * LANE
    z.LO = z.DH - z.WS
    z.W = width - z.WS
    z.HN = HEADS // 2
    z.HS = z.HN // 2 * HEAD_DIM
    z.SW = z.HS // LANE * LANE
    z.SL = up(z.HS + z.LO + z.HS - z.SW, LANE)
    z.PQ = up(3 * z.HS, LANE)
    z.QN = dp_count // 2
    z.QH = z.QN // 2
    z.QP = z.QN // 4
    z.bits = z.QN.bit_length() - 1
    z.far = z.bits > 3
    z.NB = 2 * z.QN
    blocks = 4 * z.QN
    z.r2, z.rs, z.rp, z.r1 = hidden_width // blocks, 2 * width // blocks, width // blocks, width // z.QN
    z.r2p, z.rsp, z.rpp, z.r1p = (up(v, 16) for v in (z.r2, z.rs, z.rp, z.r1))
    return z


def transpose_block(src, block, r, rp, shift, sp, total):
    span = min(up(r + LANE - 1, LANE), total)
    first = shift + block * r
    start = jnp.minimum(first // LANE * LANE, total - span)
    start = pl.multiple_of(start, LANE)
    row, lane = iota((rp, span), 0), iota((rp, span), 1)
    pick = onehot((lane == row + (first - start)) & (row < r))
    return mm_nt(pick, src[0:sp, pl.ds(start, span)]).astype(B16)


def jobs_of(z):
    rest = list(range(2, z.bits))
    near, far = [0, 1, *rest], [1, 0, *rest]
    jobs, base = [], 0
    for name, group, r, rp, start, n, w, parts, order in (
        ("2a", "2", z.r2, z.r2p, 0, 2 * TILE, TILE, 1, near),
        ("2b", "2", z.r2, z.r2p, 2 * TILE, z.D - 2 * TILE, TILE, 1, far),
        ("1a", "1", z.r1, z.r1p, 0, 2 * TILE, TILE, 1, near),
        ("1b", "1", z.r1, z.r1p, 2 * TILE, z.FH // 2 - 2 * TILE, TILE, 1, far),
        ("p", "p", z.rp, z.rpp, 0, z.D, TILE, 1, near),
        ("qa", "q", z.r1, z.r1p, 0, 512, 512, 1, near),
        ("qb", "q", z.r1, z.r1p, 512, z.PQ - 512, TILE, 1, far),
        ("s", "s", z.rs, z.rsp, 0, z.D, TILE, 1, near),
    ):
        jobs.append(
            types.SimpleNamespace(
                name=name, group=group, r=r, rp=rp, start=start, n=n, w=w, nt=n // w, parts=parts, order=order, base=base
            )
        )
        base += n // w * parts
    return jobs, base


GROUPS = "21pqs"


def landing_of(z):
    return {
        f"rv{j.name}{s}": ((j.nt,) + (2,) * (z.bits - 1 - s) + (j.rp, j.w), z.far)
        for j in jobs_of(z)[0]
        for s in range(z.bits)
    }


INS = (
    "lens", "tok", "sk", "cot", "sb", "g1", "h1", "pb", "g2", "h2", "b1", "b2", "sw", "qw", "pw", "f1", "f2",
)
LEFT_OUTS = ("LT2", "LT1", "LTq", "LTp", "LTs", "R1", "Rp", "Rq")


def any_outs(z):
    return LEFT_OUTS + tuple(n for n, (_, out) in landing_of(z).items() if out)


VMEM_OUTS = ("bo", "tg", "sg", "w2", "fr1", "wp", "frq", "ws", "vout")


def out_shapes(z):
    s = jax.ShapeDtypeStruct
    landing = {n: s(shape, B16) for n, (shape, _) in landing_of(z).items()}
    left = lambda rows: s((2, 2, 2, z.QP, rows, z.SP), B16)
    return landing | dict(
        LT2=left(z.r2p),
        LT1=left(z.r1p),
        LTq=left(z.r1p),
        LTp=left(z.rpp),
        LTs=left(z.rsp),
        R1=s((2, z.S, z.FH // 2), B16),
        Rp=s((2, z.S, z.D), B16),
        Rq=s((2, z.S, z.PQ), B16),
        bo=s((z.half, z.D), B16),
        tg=s((z.half, z.D), B16),
        sg=s((2 * z.half, z.DH), B16),
        w2=s((z.r2, z.D), F32),
        fr1=s((4, up(z.r1 // 4, 8), z.FH // 2), F32),
        wp=s((z.rp, z.D), F32),
        frq=s((4, up(z.r1 // 4, 8), z.PQ), F32),
        ws=s((z.rs, z.D), F32),
        vout=s((16, z.D), F32),
    )


def scratch_of(z):
    v, dma = pltpu.VMEM, pltpu.SemaphoreType.DMA
    jobs, tiles = jobs_of(z)
    out = dict(
        tokin=v((2, z.HP, z.D), B16),
        skin=v((2, z.S, z.W), B16),
        lent=v((2, 8, LANE), F32),
        dfin=v((2, z.S, z.D), B16),
        acc0=v((z.S, z.D), F32),
        acc1=v((z.S, z.D), F32),
        acc2=v((z.S, z.D), F32),
        acc3=v((z.HP, z.D), F32),
        psend=v((z.D // TILE, z.S, TILE), B16),
        pin0=v((z.D // TILE, z.S, TILE), B16),
        pin1=v((z.D // TILE, z.S, TILE), B16),
        pin3=v((z.HP, z.D), B16),
        pk=v((z.S, 3 * z.W), B16),
        probs=v((z.HN, z.S, z.S), B16),
        dact=v((z.S, z.FH), B16),
        dbase=v((2, z.S, z.D), B16),
        st2=v((4, 2, z.QP, z.r2p, z.SP), B16),
        st1=v((2, 2, z.QP, z.r1p, z.SP), B16),
        heads=v((z.SP, z.W), B16),
        bosum=v((z.HP, z.D), B16),
        rowv=v((8, z.D), F32),
        b1v=v((1, z.FF), F32),
        fbias=v((1, z.FH), F32),
        vb=v((3 + z.bits, 16, z.D), F32),
        vr=v((2 + z.bits, 16, z.D), F32),
    )
    for n, (shape, outside) in landing_of(z).items():
        if not outside:
            out[n] = v(shape, B16)
    out["wsem"] = dma((12,))
    out["lsem"] = dma((16,))
    out["ssem"], out["rsem"] = dma((64,)), dma((64,))
    out["semld"] = dma((len(GROUPS), 6))
    out["semgs"], out["semgr"] = dma((z.bits, tiles)), dma((z.bits, tiles))
    out["semfs"], out["semfr"] = dma((2, 4)), dma((2, 4))
    out["semvs"], out["semvr"] = dma((2 + z.bits,)), dma((2 + z.bits,))
    return out


def scope_one(z):
    v = pltpu.VMEM
    return dict(
        qwv=v((z.D, 3 * z.W), B16),
        pwv=v((z.W, z.D), B16),
        f1v=v((z.D, z.FH), B16),
        f2v=v((z.FH, z.D), B16),
        atile=v((z.S, TILE), F32),
        hidden=v((z.SP, z.FH), B16),
        normed=v((z.SP, z.D), B16),
        normed2=v((z.SP, z.D), B16),
        stq=v((2, 2, z.QP, z.r1p, z.SP), B16),
        sts=v((4, 2, z.QP, z.rsp, z.SP), B16),
    )


def scope_start(z):
    v = pltpu.VMEM
    return dict(
        tokpad=v((z.HP, z.D), B16),
        skpad=v((z.S, z.W), B16),
        xin=v((z.SP, z.D), B16),
    )


def scope_two(z):
    v = pltpu.VMEM
    jobs, _ = jobs_of(z)
    out = dict(
        dmidl=v((z.S, z.D), B16),
        dpack=v((z.S, 3 * z.W), B16),
        slab=v((2, z.S, z.PQ), B16),
        stp=v((4, 2, z.QP, z.rpp, z.SP), B16),
        slotl=v((1, 2, 2, 2, z.QP, max(z.r1p, z.r2p, z.rsp), z.SP), B16),
        slotr=v((1, 2 * z.SP, z.D), B16),
    )
    if z.far:
        out["zin"] = v((2 * z.QP, max(j.rp for j in jobs), 512), B16)
    for j in jobs:
        out["pr" + j.name] = v((j.nt,) + (2,) * z.bits + (j.rp, j.w), B16)
    return out


def scope_back(z):
    v = pltpu.VMEM
    return dict(qwb=v((z.D, 3 * z.W), B16), pwb=v((z.W, z.D), B16))


def scope_end(z):
    v = pltpu.VMEM
    fp = up(z.r1 // 4, 8)
    return dict(
        swb=v((z.D, z.D), B16),
        sumt=v((z.r1p, 512), F32),
        fs1=v((4, fp, z.FH // 2), F32),
        fsq=v((4, fp, z.PQ), F32),
    )


def kernel(z, *refs):
    scratch = scratch_of(z)
    r = types.SimpleNamespace(**dict(zip((*INS, *any_outs(z), *VMEM_OUTS, *scratch), refs, strict=True)))
    jobs, _ = jobs_of(z)
    j2a, j2b, j1a, j1b, jp, jqa, jqb, js = jobs
    d, x = lax.axis_index("dp"), lax.axis_index("seq")
    c, q = lax.rem(d, 2), d // 2
    bit = [lax.rem(q // 2**b, 2) for b in range(z.bits)]
    me = 2 * c + x
    peer, xpeer = (d + 1 - 2 * c, x), (d, 1 - x)
    across = [(d + (1 - 2 * bit[b]) * 2 ** (b + 1), x) for b in range(z.bits)]
    D, S, HP, half = z.D, z.S, z.HP, z.half
    nt = D // TILE

    def scoped(spec, body):
        def inner(*held):
            for name, ref in zip(spec, held, strict=True):
                setattr(r, name, ref)
            body()
            for name in spec:
                delattr(r, name)

        pl.run_scoped(inner, *spec.values())

    def quad(k):
        return (2 * q + k // 2, lax.rem(k, 2))

    def copy_to(src, dst, ss, rs, dev):
        return pltpu.make_async_remote_copy(
            src_ref=src, dst_ref=dst, send_sem=ss, recv_sem=rs, device_id=dev, device_id_type=MESH
        )

    used = [0]

    def slots(n):
        used[0] += n
        return used[0] - n

    def remote(src, dst, slot, dev):
        return copy_to(src, dst, r.ssem.at[slot], r.rsem.at[slot], dev)

    def wait_recv(dst, slot):
        remote(dst, dst, slot, xpeer).wait_recv()

    def wait_send(src, slot):
        remote(src, src, slot, xpeer).wait_send()

    def local(src, dst, n):
        return pltpu.make_async_copy(src, dst, r.lsem.at[n])

    def load(src, dst, n):
        return pltpu.make_async_copy(src, dst, r.wsem.at[n])

    def at16(start, n):
        return pl.ds(pl.multiple_of(start, 16), n)

    def at128(start, n):
        return pl.ds(pl.multiple_of(start, LANE), n)

    hx, hx1, hc, hc1 = (at16(HP * v, HP) for v in (x, 1 - x, c, 1 - c))

    S_LEN, S_TOK, S_SK, S_COT, S_P0, S_P1, S_P2, S_P4 = (slots(n) for n in (1, 2, 2, 3, nt, nt, nt, nt))
    S_P3, S_TS, S_TP, S_T2, S_XQ, S_X1, S_XP, S_XS, S_R1, S_RQ, S_BO = (
        slots(n) for n in (1, 3, 3, 6, 2, 2, 2, 2, 1, 1, 1)
    )

    barrier = pltpu.get_barrier_semaphore()
    for t in range(1, 4):
        pl.semaphore_signal(barrier, inc=1, device_id=quad(lax.rem(me + t, 4)), device_id_type=MESH)
    for other in across:
        pl.semaphore_signal(barrier, inc=1, device_id=other, device_id_type=MESH)
    pl.semaphore_wait(barrier, 3 + z.bits)

    def qkv_loads(dst):
        return [
            load(r.qw.at[:, at128(D * j + z.WS * c, z.W)], dst.at[:, z.W * j : z.W * (j + 1)], 1 + j) for j in range(3)
        ]

    def proj_load(dst):
        return load(r.pw.at[at16(z.WS * c, z.W), :], dst, 4)

    def partial_sums(value, mine, theirs, slot):
        def step(i):
            v = value(i)
            at = lanes_of(i)
            mine[:, at] = v
            r.psend[i] = v.astype(B16)
            remote(r.psend.at[i], theirs.at[i], slot + i, peer).start()

        loop(nt, step)

    def partial_done(theirs, slot):
        def step(i):
            remote(r.psend.at[i], theirs.at[i], slot + i, peer).wait()

        loop(nt, step)

    def spread_blocks(src, stage, rr, rrp, shift, out, slot, lslot, part=0, parts=1):
        n = z.NB // parts
        known = src.shape[1] * (part + 1) // parts

        def step(b):
            m = b // 4
            stage[lax.rem(b, 4), m // z.QP, lax.rem(m, z.QP)] = transpose_block(src, b, rr, rrp, shift, z.SP, known)

        loop(n, step, 4, part * n)
        some = slice(part, part + 1) if parts > 1 else slice(0, 2)
        for t in range(1, 4):
            k = lax.rem(me + t, 4)
            remote(stage.at[k, some], out.at[x, c, some], slot + part * 3 + t - 1, quad(k)).start()
        local(stage.at[me, some], out.at[x, c, some], lslot + part).start(priority=1)

    def spread_sent(stage, out, slot, lslot, parts=1):
        n = 2 // parts
        for i in range(3 * parts):
            wait_send(stage.at[0, 0:n], slot + i)
        for part in range(parts):
            local(stage.at[0, 0:n], out.at[x, 0, 0:n], lslot + part).wait()

    def spread_here(out, slot, part=0, parts=1):
        for i in range(3):
            wait_recv(out.at[x, 0, 0 : 2 // parts], slot + part * 3 + i)

    def whole_blocks(src, stage, out, slot, lslot):
        def step(b):
            stage[b // (2 * z.QP), lax.rem(b // z.QP, 2), lax.rem(b, z.QP)] = transpose_block(
                src, b, z.r1, z.r1p, 0, z.SP, D
            )

        loop(z.QN, step, 4)
        remote(stage.at[c], out.at[x, c], slot, xpeer).start()
        local(stage, out.at[x], lslot).start(priority=1)

    def relay(out, part, slot):
        wait_recv(out.at[1 - x, part], slot)
        remote(out.at[1 - x, part], out.at[1 - x, part], slot + 1, peer).start()

    def whole(tiles, at):
        return jnp.concatenate([tiles[t, at] for t in range(nt)], axis=1).astype(F32)

    def normalise(v, gain, shift):
        mean = jnp.mean(v, axis=-1, keepdims=True)
        centred = v - mean
        var = jnp.mean(centred * centred, axis=-1, keepdims=True)
        return centred * lax.rsqrt(var + NORM_EPS) * gain + shift

    def norm_back(v, dn, gain):
        mean = jnp.mean(v, axis=-1, keepdims=True)
        centred = v - mean
        var = jnp.mean(centred * centred, axis=-1, keepdims=True)
        rstd = lax.rsqrt(var + NORM_EPS)
        hat = centred * rstd
        dh = dn * gain
        one = jnp.mean(dh, axis=-1, keepdims=True)
        two = jnp.mean(dh * hat, axis=-1, keepdims=True)
        return rstd * (dh - one - hat * two), dn * hat

    def fold(v):
        return jnp.sum(v, axis=0, keepdims=True)

    zero = jnp.zeros((1, D), F32)
    SB, G1, H1, PB, G2, H2, B2 = range(7)

    def rowp(i):
        return r.rowv[i : i + 1, :]

    tok_self, sk_self = (c == 0) & (x == 0), (c == 1) & (x == 1)
    span = 2 * LANE
    scale = HEAD_DIM ** (-0.5)

    def head_window(h):
        first = z.LO * c + HEAD_DIM * h
        start = pl.multiple_of(jnp.minimum(first // LANE * LANE, z.W - span), LANE)
        lane = iota((1, span), 1) + start
        keep = jnp.where((lane >= first) & (lane < first + HEAD_DIM), 1.0, 0.0)
        return start, keep

    def length_here():
        return jnp.where(c == x, r.lent[0], r.lent[1])[0:1, 0:1]

    def begin():
        load(r.sw.at[at16(D * c, D)], r.f1v.at[:, 0:D], 0).start(priority=1)
        for v in qkv_loads(r.qwv):
            v.start(priority=1)
        proj_load(r.pwv).start(priority=1)
        length = r.lens[0].astype(F32)
        r.lent[0] = jnp.full((8, LANE), length, F32)
        remote(r.lent.at[0], r.lent.at[1], S_LEN, peer).start()
        spread = onehot((iota((HP, half), 0) == iota((HP, half), 1)))
        r.tokpad[...] = mm(spread, r.tok[...]).astype(B16)

        @pl.when(tok_self)
        def _():
            r.tokin[x] = r.tokpad[...]

        @pl.when(jnp.logical_not(tok_self))
        def _():
            remote(r.tokpad, r.tokin.at[x], S_TOK + x, quad(c)).start()

        row, col = iota((S, 2 * half), 0), iota((S, 2 * half), 1)
        pick = onehot(((row < half) & (row == col)) | ((row >= HP) & (row < HP + half) & (col == row - (HP - half))))
        shift = onehot(iota((z.DH, z.W), 1) == iota((z.DH, z.W), 0) + z.LO * x)
        r.skpad[...] = mm(mm(pick, r.sk[...]).astype(B16), shift).astype(B16)

        @pl.when(sk_self)
        def _():
            r.skin[x] = r.skpad[...]

        @pl.when(jnp.logical_not(sk_self))
        def _():
            remote(r.skpad, r.skin.at[x], S_SK + x, quad(2 + c)).start()

        own_row = iota((HP, 1), 0)
        live = (own_row < half) & ((own_row + half * x).astype(F32) < length)
        r.dfin[c, hx] = jnp.where(live, mm(spread, r.cot[...]), 0.0).astype(B16)

        for ref in (r.xin, r.normed, r.normed2, r.hidden):
            ref[S:, :] = jnp.zeros((z.SP - S, ref.shape[1]), B16)
        r.heads[...] = jnp.zeros(r.heads.shape, B16)
        for i, ref in enumerate((r.sb, r.g1, r.h1, r.pb, r.g2, r.h2, r.b2)):
            r.rowv[i : i + 1, :] = ref[...].astype(F32).reshape(1, D)
        r.b1v[...] = r.b1[...].astype(F32).reshape(1, z.FF)

        for h in range(2):
            @pl.when((c == 0) & jnp.logical_not(tok_self & (h == 0)))
            def _(h=h):
                wait_recv(r.tokin.at[h], S_TOK + h)

            @pl.when((c == 1) & jnp.logical_not(sk_self & (h == 1)))
            def _(h=h):
                wait_recv(r.skin.at[h], S_SK + h)

        remote(r.dfin.at[c, hx], r.dfin.at[c, hx], S_COT, xpeer).start()
        remote(r.dfin.at[c, hx], r.dfin.at[c, hx], S_COT + 1, peer).start()

        @pl.when(c == 0)
        def _():
            for h in range(2):
                r.xin[h * HP : (h + 1) * HP, :] = r.tokin[h]

        @pl.when(c == 1)
        def _():
            r.xin[0:S, 0 : z.WS] = r.skin[0, :, 0 : z.WS]
            r.xin[0:S, z.WS : z.W] = r.skin[0, :, z.WS : z.W] + r.skin[1, :, 0 : z.W - z.WS]
            r.xin[0:S, z.W : D] = r.skin[1, :, z.W - z.WS : z.W]

        load(r.sw.at[at16(D * c, D)], r.f1v.at[:, 0:D], 0).wait()
        partial_sums(lambda i: mm(r.xin[0:S], r.f1v[:, lanes_of(i)]), r.acc0, r.pin0, S_P0)
        spread_blocks(r.xin, r.sts, z.rs, z.rsp, 0, r.LTs, S_TS, 0)

        @pl.when(jnp.logical_not(tok_self))
        def _():
            wait_send(r.tokpad, S_TOK + x)

        @pl.when(jnp.logical_not(sk_self))
        def _():
            wait_send(r.skpad, S_SK + x)

    def ff_loads():
        return [load(r.f1.at[:, at128(z.FH * c, z.FH)], r.f1v, 5), load(r.f2.at[at16(z.FH * c, z.FH), :], r.f2v, 6)]

    def forward():
        scoped(scope_start(z), begin)
        for v in ff_loads():
            v.start(priority=1)
        partial_done(r.pin0, S_P0)

        def norm_one(i):
            at = rows_of(i)
            v = r.acc0[at] + whole(r.pin0, at) + rowp(SB)
            r.acc0[at] = v
            r.normed[at] = normalise(v, rowp(G1), rowp(H1)).astype(B16)

        loop(S // ROWS, norm_one, S // ROWS)
        for v in qkv_loads(r.qwv):
            v.wait()

        def qkv_tile(i):
            r.pk[:, lanes_of(i)] = mm(r.normed[0:S], r.qwv[:, lanes_of(i)]).astype(B16)

        loop(3 * z.W // TILE, qkv_tile)

        wait_recv(r.dfin.at[c, hx1], S_COT)
        remote(r.dfin.at[c, hx1], r.dfin.at[c, hx1], S_COT + 2, peer).start()

        wait_recv(r.lent.at[1], S_LEN)
        slot_col = iota((1, S), 1)
        slot_of = jnp.where(slot_col < HP, slot_col, slot_col - (HP - half))
        key_ok = ((slot_col < half) | ((slot_col >= HP) & (slot_col < HP + half))) & (
            slot_of.astype(F32) < length_here()
        )

        def head_forward(h):
            start, keep = head_window(h)
            query = r.pk[:, pl.ds(start, span)] * keep.astype(B16)
            key = r.pk[:, at128(z.W + start, span)]
            value = r.pk[:, at128(2 * z.W + start, span)]
            scores = jnp.where(key_ok, mm_nt(query, key) * scale, MASKED)
            top = jnp.max(scores, axis=-1, keepdims=True)
            e = jnp.exp(scores - top)
            probs = (e * (1.0 / jnp.sum(e, axis=-1, keepdims=True))).astype(B16)
            r.probs[h] = probs
            at = pl.ds(start, span)
            r.heads[0:S, at] = r.heads[0:S, at] + (mm(probs, value) * keep).astype(B16)

        loop(z.HN, head_forward, 2)

        proj_load(r.pwv).wait()
        partial_sums(lambda i: mm(r.heads[0:S], r.pwv[:, lanes_of(i)]), r.acc1, r.pin1, S_P1)
        whole_blocks(r.normed, r.stq, r.LTq, S_XQ, 1)
        partial_done(r.pin1, S_P1)

        def norm_two(i):
            at = rows_of(i)
            v = r.acc0[at] + r.acc1[at] + whole(r.pin1, at) + rowp(PB)
            r.acc1[at] = v
            r.normed2[at] = normalise(v, rowp(G2), rowp(H2)).astype(B16)

        loop(S // ROWS, norm_two, S // ROWS)

        whole_blocks(r.normed2, r.st1, r.LT1, S_X1, 4)
        wait_recv(r.dfin.at[1 - c, hx], S_COT + 1)
        wait_recv(r.dfin.at[1 - c, hx1], S_COT + 2)
        for v in ff_loads():
            v.wait()

        def hidden_tile(i):
            at = lanes_of(i)
            a = mm(r.normed2[0:S], r.f1v[:, at]) + r.b1v[:, at128(z.FH * c + i * TILE, TILE)]
            dh = mm_nt(r.dfin[x], r.f2v[rows_of(i, TILE), :])
            cdf = 0.5 * (1.0 + lax.erf(a * (2.0**-0.5)))
            pdf = jnp.exp(-0.5 * a * a) * (0.5 / jnp.pi) ** 0.5
            r.hidden[0:S, at] = (a * cdf).astype(B16)
            da = dh * (cdf + a * pdf)
            r.dact[:, at] = da.astype(B16)
            r.fbias[:, at] = fold(da)

        tiles, fq = z.FH // TILE // 2, z.FH // 2
        loop(tiles, lambda i: hidden_tile(tiles * (1 - x) + i), tiles)
        remote(r.dact.at[:, at128(fq * (1 - x), fq)], r.R1.at[x], S_R1, xpeer).start()
        relay(r.LTq, c, S_XQ)
        relay(r.LT1, c, S_X1)
        loop(tiles, lambda i: hidden_tile(tiles * x + i), tiles)
        partial_sums(lambda i: mm_nt(r.dact[...], r.f1v[rows_of(i, TILE), :]), r.acc2, r.pin0, S_P2)
        spread_blocks(r.hidden, r.st2, z.r2, z.r2p, 0, r.LT2, S_T2, 8)
        local(r.dact.at[:, at128(fq * x, fq)], r.R1.at[x], 3).start(priority=1)

        def result_tile(i):
            at = lanes_of(i)
            r.atile[...] = mm(r.hidden[0:S], r.f2v[:, at])
            r.acc3[:, at] = r.atile[hc]
            r.tokin[0, :, at] = r.atile[hc1].astype(B16)

        loop(nt, result_tile)
        remote(r.tokin.at[0], r.pin3, S_P3, peer).start()
        spread_sent(r.sts, r.LTs, S_TS, 0)
        wait_send(r.stq.at[c], S_XQ)
        local(r.stq, r.LTq.at[x], 1).wait()

    def ref(kind, j):
        return getattr(r, kind + j.name)

    def tile(j, i):
        return at128(j.start + i * j.w, j.w)

    def group_loads(j, part):
        n = GROUPS.index(j.group)
        s = n % r.slotl.shape[0]
        left = getattr(r, "LT" + j.group)
        right = {"2": r.dfin, "1": r.R1, "p": r.Rp, "q": r.Rq, "s": r.dbase}[j.group]
        some = slice(0, 2) if part is None else slice(part, part + 1)
        for i in range(2):
            yield pltpu.make_async_copy(
                left.at[i, :, some], r.slotl.at[s, i, :, some, :, 0 : j.rp], r.semld.at[n, 2 * (part or 0) + i]
            )
            if not part:
                yield pltpu.make_async_copy(
                    right.at[i], r.slotr.at[s, i * z.SP : i * z.SP + S, 0 : right.shape[-1]], r.semld.at[n, 4 + i]
                )

    def kept(j, s, keep, part=None):
        at = [slice(None)] * z.bits
        for b in j.order[:s]:
            at[z.bits - 1 - b] = bit[b]
        b = j.order[s]
        at[z.bits - 1 - b] = bit[b] if keep else 1 - bit[b]
        if part is not None:
            at[1] = slice(part, part + 1)
        return tuple(at)

    def landed(j, s):
        return getattr(r, f"rv{j.name}{s}")

    def half_copy(j, s, i, part=0):
        split = s == 0 and j.parts > 1
        src = ref("pr", j).at[(i, *kept(j, s, False, part if split else None))]
        dst = landed(j, s)
        lead = (i, slice(None), slice(part, part + 1)) if split else (i,)
        n = j.base + part * j.nt + i
        return copy_to(src, dst.at[lead], r.semgs.at[s, n], r.semgr.at[s, n], across[j.order[s]])

    def prep(j, part=None):
        for v in group_loads(j, part):
            v.start(priority=1)

    def ready(j, part=None):
        for v in group_loads(j, part):
            v.wait()

    def products(j, part=0):
        s = GROUPS.index(j.group) % r.slotl.shape[0]

        def step(i):
            at = tile(j, i)
            if j.parts > 1:
                left = [r.slotl[s, n, :, part, :, 0 : j.rp] for n in range(2)]
                to = (slice(None), part)
            else:
                left = [r.slotl[s, n, :, :, :, 0 : j.rp] for n in range(2)]
                to = ()
            left = [v.reshape(z.QN // j.parts * j.rp, z.SP) for v in left]
            out = mm(jnp.concatenate(left, axis=1), r.slotr[s, :, at])
            shape = (2,) * (z.bits - (j.parts > 1)) + (j.rp, j.w)
            ref("pr", j)[(i, *to)] = out.astype(B16).reshape(shape)
            half_copy(j, 0, i, part).start()

        loop(j.nt, step)

    def sums(j, s, store=None):
        def step(i):
            at = tile(j, i)
            for part in range(j.parts if s == 0 else 1):
                half_copy(j, s, i, part).wait_recv()
            here = (i, *kept(j, s, True))
            theirs = landed(j, s)
            if z.far:
                n = 2 ** (z.bits - 1 - s)
                stage = r.zin.at[0:n, 0 : j.rp, 0 : j.w]
                for k in range(n):
                    pick = tuple(k // 2**b % 2 for b in reversed(range(z.bits - 1 - s)))
                    fetch = local(theirs.at[(i, *pick)], stage.at[k], 15)
                    fetch.start()
                    fetch.wait()
                piece = stage[...].reshape(theirs.shape[1:])
            else:
                piece = theirs[i]
            total = ref("pr", j)[here].astype(F32) + piece.astype(F32)
            if s < z.bits - 1:
                ref("pr", j)[here] = total.astype(B16)
                half_copy(j, s + 1, i).start()
            else:
                store(at, total)

        loop(j.nt, step)

    def more_sums(j):
        for s in range(2, z.bits - 1):
            sums(j, s)

    def sums_sent(j):
        def step(i):
            for s in range(z.bits):
                for part in range(j.parts if s == 0 else 1):
                    half_copy(j, s, i, part).wait_send()

        loop(j.nt, step)

    rq = z.r1 // 4

    def fix_copy(n, g, t):
        k = lax.rem(me + t, 4)
        src, dst = getattr(r, "fs" + g), getattr(r, "fr" + g)
        return copy_to(src.at[k], dst.at[me], r.semfs.at[n, t - 1], r.semfr.at[n, t - 1], quad(k))

    def fix_start(n, g):
        for t in range(1, 4):
            fix_copy(n, g, t).start()
        getattr(r, "fr" + g)[me] = getattr(r, "fs" + g)[me]

    def fix_wait(n, g):
        for t in range(1, 4):
            fix_copy(n, g, t).wait()

    def direct(out):
        def store(at, total):
            out[:, at] = total[0 : out.shape[0]]

        return store

    def summed(out):
        def store(at, total):
            w = total.shape[1]
            r.sumt[:, 0:w] = total
            for k in range(4):
                out[k, 0:rq, at] = r.sumt[k * rq : (k + 1) * rq, 0:w]

        return store

    v_devs = (peer, xpeer, *across)

    def v_copy(s):
        return copy_to(r.vb.at[s], r.vr.at[s], r.semvs.at[s], r.semvr.at[s], v_devs[s])

    def v_step(s):
        if s > 0:
            v_copy(s - 1).wait()
            r.vb[s] = r.vb[s - 1] + r.vr[s - 1]
        if s < len(v_devs):
            v_copy(s).start()

    def back():
        for v in qkv_loads(r.qwb):
            v.start(priority=1)
        proj_load(r.pwb).start(priority=1)
        for s in range(r.slotr.shape[0]):
            for i in range(2):
                r.slotr[s, i * z.SP + S : (i + 1) * z.SP, :] = jnp.zeros((z.SP - S, D), B16)
        r.dpack[...] = jnp.zeros(r.dpack.shape, B16)
        partial_done(r.pin0, S_P2)

        def norm_two_back(i, sums):
            at = rows_of(i)
            dn = r.acc2[at] + whole(r.pin0, at)
            dv, dg = norm_back(r.acc1[at], dn, rowp(G2))
            df = r.dfin[x, at].astype(F32)
            dm = df + dv
            r.acc2[at] = dm
            r.dmidl[at] = dm.astype(B16)
            return sums[0] + fold(dg), sums[1] + fold(dn), sums[2] + fold(df), sums[3] + fold(dm)

        dg2, dh2, db2, dpb = lax.fori_loop(0, S // ROWS, norm_two_back, (zero, zero, zero, zero), unroll=S // ROWS)
        local(r.dmidl, r.Rp.at[x], 6).start(priority=1)
        wait_recv(r.LT1.at[1 - x, 1 - c], S_X1 + 1)
        local(r.st1, r.LT1.at[x], 4).wait()
        wait_recv(r.R1.at[1 - x], S_R1)
        local(r.R1.at[x], r.R1.at[x], 3).wait()
        prep(j1a)
        r.vb[0] = jnp.zeros((16, D), F32)
        first = jnp.where(c == 0, 1.0, 0.0)
        for i, v in ((3, dpb), (4, dg2), (5, dh2), (6, db2)):
            r.vb[0, i : i + 1, :] = v * first
        for j in range(z.FH // D):
            v = r.fbias[:, j * D : (j + 1) * D]
            r.vb[0, 8 + j : 9 + j, :] = v * first
            r.vb[0, 10 + j : 11 + j, :] = v * (1.0 - first)

        proj_load(r.pwb).wait()
        r.skin[0] = mm_nt(r.dmidl[...], r.pwb[...]).astype(B16)
        ready(j1a)
        products(j1a)
        products(j1b)

        def head_backward(h):
            start, keep = head_window(h)
            low = keep.astype(B16)
            at_q, at_k, at_v = pl.ds(start, span), at128(z.W + start, span), at128(2 * z.W + start, span)
            query, key, value = r.pk[:, at_q], r.pk[:, at_k], r.pk[:, at_v]
            dh = r.skin[0, :, at_q]
            probs = r.probs[h]
            dp = mm_nt(dh * low, value)
            pf = probs.astype(F32)
            delta = jnp.sum(dp * pf, axis=-1, keepdims=True)
            ds = (pf * (dp - delta) * scale).astype(B16)
            r.dpack[:, at_q] = r.dpack[:, at_q] + (mm(ds, key) * keep).astype(B16)
            r.dpack[:, at_k] = r.dpack[:, at_k] + (mm_tn(ds, query) * keep).astype(B16)
            r.dpack[:, at_v] = r.dpack[:, at_v] + (mm_tn(probs, dh) * keep).astype(B16)

        def slab_of(mine, part):
            first = z.LO * c + (z.HS - z.SW) * part
            row, lane = iota((z.SL, z.SL), 0), iota((z.SL, z.SL), 1)
            out = []
            for t in range(3):
                to = z.HS * t // LANE * LANE
                move = onehot((row - first == lane - (z.HS * t - to)) & (row >= first) & (row < first + z.HS))
                out.append((to, mm(r.dpack[:, at128(z.W * t + z.SW * part, z.SL)], move).astype(B16)))
            for at in range(0, z.PQ, LANE):
                held = [v[:, at - to : at - to + LANE] for to, v in out if to <= at < to + z.SL]
                r.slab[mine, :, at : at + LANE] = held[0] if len(held) == 1 else held[0] + held[1]

        nh = z.HN // 2
        loop(nh, lambda i: head_backward(nh * (1 - x) + i), 2)
        slab_of(0, 1 - x)
        remote(r.slab.at[0], r.Rq.at[x], S_RQ, xpeer).start()
        remote(r.dmidl.at[hc], r.Rp.at[x, hc], S_XP, xpeer).start()
        block_out()
        spread_here(r.LT2, S_T2)
        local(r.st2.at[0], r.LT2.at[x, 0], 8).wait()
        prep(j2a)
        ready(j2a)
        products(j2a)
        products(j2b)
        loop(nh, lambda i: head_backward(nh * x + i), 2)
        for v in qkv_loads(r.qwb):
            v.wait()
        partial_sums(lambda i: mm_nt(r.dpack[...], r.qwb[rows_of(i, TILE), :]), r.acc1, r.pin1, S_P4)
        slab_of(1, x)
        local(r.slab.at[1], r.Rq.at[x], 7).start(priority=1)
        spread_blocks(r.heads, r.stp, z.rp, z.rpp, z.LO * c, r.LTp, S_TP, 2)
        sums(j1a, 0)
        sums(j1b, 0)
        wait_recv(r.LTq.at[1 - x, 1 - c], S_XQ + 1)
        wait_recv(r.Rq.at[1 - x], S_RQ)
        local(r.Rq.at[x], r.Rq.at[x], 7).wait()
        prep(jqa)
        relay(r.Rp, hc, S_XP)

    def block_out():
        wait_recv(r.pin3, S_P3)
        slot_row = iota((HP, 1), 0)
        out_ok = (slot_row < half) & ((slot_row + half * c).astype(F32) < length_here())
        total = r.acc1[hc] + r.acc3[...] + r.pin3[...].astype(F32) + rowp(B2)
        r.tokin[1] = jnp.where(out_ok, total, 0.0).astype(B16)

        @pl.when(c == x)
        def _():
            r.bosum[...] = r.tokin[1]

    def finish():
        weight = [
            load(r.sw.at[0:D], r.swb, 8),
            load(r.sw.at[at16(D + z.DH * x, z.DH)], r.swb.at[0 : z.DH], 9),
        ]
        weight[0].start(priority=1)
        partial_done(r.pin1, S_P4)

        def norm_one_back(i, sums):
            at = rows_of(i)
            dn = r.acc1[at] + whole(r.pin1, at)
            dv, dg = norm_back(r.acc0[at], dn, rowp(G1))
            db = r.acc2[at] + dv
            r.dbase[x, at] = db.astype(B16)
            return sums[0] + fold(dg), sums[1] + fold(dn), sums[2] + fold(db)

        dg1, dh1, dsb = lax.fori_loop(0, S // ROWS, norm_one_back, (zero, zero, zero), unroll=S // ROWS)
        first = jnp.where(c == 0, 1.0, 0.0)
        for i, v in enumerate((dsb, dg1, dh1)):
            r.vb[0, i : i + 1, :] = v * first
        v_step(0)

        remote(r.dbase.at[x, hc], r.dbase.at[x, hc], S_XS, xpeer).start()
        ready(jqa)
        products(jqa)
        products(jqb)
        wait_recv(r.Rp.at[1 - x, hc1], S_XP + 1)
        local(r.dmidl, r.Rp.at[x], 6).wait()
        spread_here(r.LTp, S_TP)
        spread_sent(r.stp, r.LTp, S_TP, 2)
        prep(jp)
        v_step(1)
        sums(j2b, 0)
        sums(j1b, 1)
        ready(jp)
        products(jp)
        sums(j1a, 1)
        relay(r.dbase, hc, S_XS)
        spread_here(r.LTs, S_TS)
        sums(j2a, 0)
        wait_recv(r.dbase.at[1 - x, hc1], S_XS + 1)
        prep(js)
        v_step(2)

        @pl.when(c != x)
        def _():
            remote(r.tokin.at[1], r.bosum, S_BO, (2 * q + x, c)).start()

        ready(js)
        products(js)
        more_sums(j1a)
        more_sums(j1b)
        v_step(3)
        sums(j2b, 1)
        sums(jp, 0)
        sums(jqb, 0)
        sums(j1b, z.bits - 1, summed(r.fs1))
        weight[0].wait()
        r.tg[...] = mm_nt(r.dbase[c, hx], r.swb[...]).astype(B16)[0:half]
        weight[1].start(priority=1)
        v_step(4)
        sums(j1a, z.bits - 1, summed(r.fs1))
        fix_start(0, "1")
        sums(j2a, 1)
        sums(jqa, 0)
        more_sums(j2a)
        more_sums(j2b)
        sums(j2b, z.bits - 1, direct(r.w2))
        weight[1].wait()
        sg = mm_nt(r.dbase[c], r.swb[0 : z.DH, :]).astype(B16)
        row, col = iota((2 * half, S), 0), iota((2 * half, S), 1)
        back_rows = onehot(((row < half) & (row == col)) | ((row >= half) & (col == row + (HP - half))))
        r.sg[...] = mm(back_rows, sg).astype(B16)
        for s in range(5, len(v_devs) + 1):
            v_step(s)
        r.vout[...] = r.vb[len(v_devs)]
        sums(jqb, 1)
        more_sums(jqb)
        sums(jp, 1)
        more_sums(jp)
        sums(js, 0)
        sums(j2a, z.bits - 1, direct(r.w2))

        @pl.when(c == x)
        def _():
            r.bosum[...] = r.tokin[1]

        @pl.when(c != x)
        def _():
            remote(r.tokin.at[1], r.bosum, S_BO, (2 * q + x, c)).wait()

        r.bo[...] = r.bosum[0:half]
        sums(jqa, 1)
        more_sums(jqa)
        sums(jqb, z.bits - 1, summed(r.fsq))
        fix_wait(0, "1")
        sums(jp, z.bits - 1, direct(r.wp))
        sums(js, 1)
        more_sums(js)
        sums(jqa, z.bits - 1, summed(r.fsq))
        fix_start(1, "q")
        sums(js, z.bits - 1, direct(r.ws))
        fix_wait(1, "q")

        wait_send(r.lent.at[0], S_LEN)
        for j in range(3):
            wait_send(r.dfin.at[c, hx], S_COT + j)
        for j in range(3):
            wait_send(r.st2.at[0], S_T2 + j)
        wait_send(r.tokin.at[0], S_P3)
        wait_send(r.st1.at[c], S_X1)
        wait_send(r.dmidl.at[hc], S_XP)
        wait_send(r.dbase.at[x, hc], S_XS)
        wait_send(r.LTq.at[1 - x, c], S_XQ + 1)
        wait_send(r.LT1.at[1 - x, c], S_X1 + 1)
        wait_send(r.Rp.at[1 - x, hc], S_XP + 1)
        wait_send(r.dbase.at[1 - x, hc], S_XS + 1)
        wait_send(r.R1.at[x], S_R1)
        wait_send(r.slab.at[0], S_RQ)
        for j in jobs:
            sums_sent(j)

    def backward():
        scoped(scope_back(z), back)
        scoped(scope_end(z), finish)

    scoped(scope_one(z), forward)
    scoped(scope_two(z), backward)


def call(z, *args):
    outs = out_shapes(z)
    anywhere, vmem = pl.BlockSpec(memory_space=pl.ANY), pl.BlockSpec(memory_space=pltpu.VMEM)
    names = (*any_outs(z), *VMEM_OUTS)
    res = pl.pallas_call(
        functools.partial(kernel, z),
        out_shape=[outs[n] for n in names],
        in_specs=[pl.BlockSpec(memory_space=pltpu.SMEM), *([vmem] * 11), *([anywhere] * 5)],
        out_specs=[anywhere] * len(any_outs(z)) + [vmem] * len(VMEM_OUTS),
        scratch_shapes=list(scratch_of(z).values()),
        compiler_params=pltpu.CompilerParams(
            collective_id=0, has_side_effects=True, vmem_limit_bytes=VMEM_BYTES
        ),
        name="block",
    )(*args)
    return dict(zip(names, res))


def place(z, bo, tg, sg, w2, fr1, wp, frq, ws, vout, *outs):
    (bo_o, tg_o, sg_o, ws_o, sb_o, g1_o, h1_o, wq_o, wp_o, pb_o, g2_o, h2_o, w1_o, b1_o, w2_o, b2_o) = outs
    for src, dst in ((bo, bo_o), (tg, tg_o), (sg, sg_o), (ws, ws_o), (wp, wp_o), (w2, w2_o)):
        dst[...] = src[...]
    rq, fq = z.r1 // 4, z.FH // 2
    for k in range(4):
        w1_o[:, k * fq : (k + 1) * fq] = fr1[k, 0:rq]
    for t in range(3):
        wq_o[:, t * z.D : (t + 1) * z.D] = jnp.concatenate(
            [frq[k, 0:rq, t * z.HS : (t + 1) * z.HS] for k in range(4)], axis=1
        )
    block = 2 * lax.axis_index("dp") + lax.axis_index("seq")

    def take(v, first, n):
        pick = jnp.where(iota((z.D, n), 0) == iota((z.D, n), 1) + first, 1.0, 0.0)
        return lax.dot_general(
            v, pick, (((1,), (0,)), ((), ())), preferred_element_type=F32, precision=lax.Precision.HIGHEST
        )

    own = take(vout[0:8], block * z.rp, z.rp)
    for i, dst in enumerate((sb_o, g1_o, h1_o, pb_o, g2_o, h2_o, b2_o)):
        dst[...] = own[i : i + 1, :].reshape(z.rp)
    per = z.D // z.r2
    row = iota((8, z.D), 0)
    held = jnp.where(row == block // per, vout[8:16], 0.0)
    b1_o[...] = jnp.sum(take(held, lax.rem(block, per) * z.r2, z.r2), axis=0, keepdims=True).reshape(z.r2)


def call_place(z, g):
    s = jax.ShapeDtypeStruct
    one = s((z.rp,), F32)
    vmem = pl.BlockSpec(memory_space=pltpu.VMEM)
    res = [
        s((z.half, z.D), B16), s((z.half, z.D), B16), s((2 * z.half, z.DH), B16), s((z.rs, z.D), F32), one, one, one,
        s((z.r1 // 4, 3 * z.D), F32), s((z.rp, z.D), F32), one, one, one, s((z.r1 // 4, z.FF), F32), s((z.r2,), F32),
        s((z.r2, z.D), F32), one,
    ]
    return pl.pallas_call(
        functools.partial(place, z),
        out_shape=res,
        in_specs=[vmem] * len(VMEM_OUTS),
        out_specs=[vmem] * len(res),
        compiler_params=pltpu.CompilerParams(vmem_limit_bytes=VMEM_BYTES),
        name="place",
    )(*(g[n] for n in VMEM_OUTS))


def shards(tokens, skip_feats, lengths, cotangent, skip_weight, skip_bias, norm1_gain, norm1_bias, qkv_weight,
           proj_weight, proj_bias, norm2_gain, norm2_bias, fc1_weight, fc1_bias, fc2_weight, fc2_bias):
    dp_count = lax.axis_size("dp")
    half, width = tokens.shape[1:]
    z = sizes(half, width, fc1_weight.shape[1], dp_count)
    g = call(z, lengths, tokens[0], skip_feats[0], cotangent[0], skip_bias, norm1_gain, norm1_bias, proj_bias,
             norm2_gain, norm2_bias, fc1_bias, fc2_bias, skip_weight, qkv_weight, proj_weight, fc1_weight, fc2_weight)
    out = call_place(z, g)
    return (*(v[None] for v in out[:3]), *out[3:])


def solution(mesh):
    placed = (P("dp", "seq", None), P("dp", None, "seq"), P("dp"), P("dp", "seq", None), *([P()] * 13))
    both = ("dp", "seq")
    return jax.shard_map(
        shards, mesh=mesh, in_specs=placed,
        out_specs=(P("dp", "seq", None), P("dp", "seq", None), P("dp", None, "seq"), P(both, None), P(both), P(both),
                   P(both), P(both, None), P(both, None), P(both), P(both), P(both), P(both, None), P(both),
                   P(both, None), P(both)),
        check_vma=False,
    )
```
